512 devices in a mesh: cell: 64 (over z, x, core), gene: 8 (over y).
Axes of the slice: x: 4, y: 8, z: 8, core: 2. Of those that a mesh axis runs over, the one named last changes fastest.
Arguments:
- expression: bfloat16 [36864, 4096], P('cell', 'gene'), may hold values from -6 to 6
- gene_mean: float32 [4096], P('gene'), may hold values from -0.5 to 0.5
- loadings: bfloat16 [4096, 256], P('gene'), may hold values from -0.09375 to 0.09375
- nbr_index: int32 [36864, 30], P('cell'), may hold values from 0 to 36863, as said below
- nbr_count: int32 [36864], P('cell'), may hold values from 8 to 30
- nbr_weight: float32 [36864, 30], P('cell'), may hold values from 0.1 to 1
- batch: int32 [36864], P('cell'), may hold values from 0 to 15
- centroids: float32 [1000, 256], replicated, may hold values from -6 to 6
Outputs:
- smooth: float32 [36864, 256], P('cell', 'gene')
- new_centroids: float32 [1000, 256], replicated
- final_obs: float32 [1000, 16], replicated
The draws below stay inside these ranges and needn't reach their ends.
Inputs may be any that keep to these rules, and one draw needn't show every extreme that they name: `nbr_index`: every entry differs from its row's cell index by 1 to 576, and the distance 576 occurs.
All inputs are finite; a program needn't handle non-finite values.
Results may differ from the reference program's by a relative error of at most 0.0022.
The reference program's roundings to bfloat16 on the way (of `unit_rows`, `cent_unit` and `response`) count: a program that leaves them out, or rounds other values in their place, can miss the bound.
Values sent between devices are 32-bit elements; how exact they have to be, the bound alone decides.
A program may use at most 64 MiB of HBM per device.

```python
import math
import jax
import jax.numpy as jnp
from jax import lax

G = 4096
P_SIZE = 256
K = 1000
B = 16
NBR = 30
DIFF_STEPS = 3
CELL_DEV = 576
CELLS = 36864
SPAN = 576
N_CELL = 64


def draw_expression(key, part):
    cell_total = CELL_DEV * N_CELL
    run_length = 4 * CELL_DEV
    run_total = cell_total // run_length
    profile = jax.random.normal(jax.random.fold_in(key, 41), (run_total, 1, G), jnp.float32)
    noise = jax.random.normal(jax.random.fold_in(key, 42), (run_total, run_length, G), jnp.float32)
    whole = jnp.clip(profile + noise, -6.0, 6.0)
    return whole.reshape(cell_total, G).astype(jnp.bfloat16)


def draw_batch(key, part):
    cell_total = CELL_DEV * N_CELL
    position = jnp.arange(cell_total, dtype=jnp.int32)
    run_number = position // (4 * CELL_DEV)
    offset = jax.random.randint(jax.random.fold_in(key, 31), (cell_total,), 0, 3)
    label = (2 * run_number + offset) % B
    label = jnp.where(position % 8 == 0, position // 8 % B, label)
    return label.astype(jnp.int32)


def draw_nbr_index(key, part):
    cell_total = CELL_DEV * N_CELL
    position = jnp.arange(cell_total, dtype=jnp.int32)[:, None]
    magnitude = jax.random.randint(jax.random.fold_in(key, 11), (cell_total, NBR), 1, SPAN + 1)
    signs = jax.random.randint(jax.random.fold_in(key, 12), (cell_total, NBR), 0, 2) * 2 - 1
    offset = magnitude * signs
    first_slot = jnp.arange(NBR, dtype=jnp.int32)[None, :] == 0
    block_head = position % CELL_DEV == 0
    offset = jnp.where(first_slot & block_head, SPAN, offset)
    target = position + offset
    outside = (target < 0) | (target >= cell_total)
    target = jnp.where(outside, position - offset, target)
    return target.astype(jnp.int32)


def draw_nbr_count(key, part):
    cell_total = CELL_DEV * N_CELL
    position = jnp.arange(cell_total, dtype=jnp.int32)
    counts = jax.random.randint(jax.random.fold_in(key, 21), (cell_total,), 8, NBR + 1)
    return jnp.where(position % 4 == 0, NBR, counts).astype(jnp.int32)


def steps_of(own_key, dims, pieces, least, high):
    gain, own = 1.0, jax.random.fold_in(own_key, 6)
    for axis_at, shards_of in pieces:
        steps = jnp.exp(jax.random.uniform(jax.random.fold_in(own, axis_at), (shards_of,), jnp.float32, least / len(pieces), high / len(pieces)))
        gain = gain * jnp.repeat(steps, dims[axis_at] // shards_of).reshape([-1 if axis == axis_at else 1 for axis in range(len(dims))])
    return gain


def bell_draw(stream_key, shape, scale, most, pieces=(), kind=jnp.bfloat16):
    values = jax.random.normal(stream_key, shape, jnp.float32) * scale
    if len(pieces) > 0:
        values = steps_of(stream_key, shape, pieces, -0.22, 0.18) * values
    return jnp.clip(values, min=-most, max=most).astype(kind)


def setup_inputs(seed: int = 0) -> dict:
    splits = jax.random.split(jax.random.key(seed), 9)
    expression = draw_expression(jax.random.fold_in(splits[8], 71), 0)
    gene_mean = jnp.clip(jax.random.uniform(splits[1], (G,), jnp.float32, -0.5, 0.5) * steps_of(splits[1], (G,), ((0, 8),), -0.4, 0.0), -0.5, 0.5)
    loadings = bell_draw(splits[2], (G, P_SIZE), G ** -0.5, 0.09375, ((0, 8),))
    nbr_index = draw_nbr_index(jax.random.fold_in(splits[8], 71), 0)
    nbr_count = draw_nbr_count(jax.random.fold_in(splits[8], 71), 0)
    nbr_weight = jnp.clip(jnp.exp(math.log(1.0) - 2.3025851 * jax.random.uniform(splits[5], (CELLS, NBR), jnp.float32) ** steps_of(splits[5], (CELLS, NBR), ((0, 64),), -0.2, 0.2)), 0.1, 1.0)
    batch = draw_batch(jax.random.fold_in(splits[8], 71), 0)
    centroids = bell_draw(splits[7], (K, P_SIZE), 1.0, 6.0, (), jnp.float32)
    return dict(expression=expression, gene_mean=gene_mean, loadings=loadings, nbr_index=nbr_index, nbr_count=nbr_count, nbr_weight=nbr_weight, batch=batch, centroids=centroids)


EPSILON = 1e-06
SIGMA_SCALE = 0.1

def diffuse_all(state_field, nbr_index, weights, denominator):

    def add_slot(slot, total_sum):
        column = lax.dynamic_slice_in_dim(nbr_index, slot, 1, 1)[:, 0]
        weight = lax.dynamic_slice_in_dim(weights, slot, 1, 1)
        return total_sum + weight * jnp.take(state_field, column, axis=0)
    total_sum = lax.fori_loop(0, NBR, add_slot, state_field)
    return total_sum / denominator[:, None]

def reference(expression, gene_mean, loadings, nbr_index, nbr_count, nbr_weight, batch, centroids):
    mean_proj = jnp.dot(gene_mean, loadings.astype(jnp.float32), precision=lax.Precision.HIGHEST)
    state_field = jnp.dot(expression, loadings, preferred_element_type=jnp.float32) - mean_proj[None, :]
    live_slots = jnp.arange(NBR)[None, :] < nbr_count[:, None]
    weights = jnp.where(live_slots, nbr_weight, jnp.float32(0.0))
    denominator = 1.0 + lax.optimization_barrier(jnp.sum(weights, axis=1))
    for repeat_step in range(DIFF_STEPS):
        state_field = diffuse_all(state_field, nbr_index, weights, denominator)
    smooth = state_field
    row_norm = jnp.sqrt(lax.optimization_barrier(jnp.sum(smooth * smooth, axis=1, keepdims=True)) + EPSILON)
    unit_rows = (smooth / row_norm).astype(jnp.bfloat16)
    cent_norm = jnp.sqrt(lax.optimization_barrier(jnp.sum(centroids * centroids, axis=1, keepdims=True)) + EPSILON)
    cent_unit = (centroids / cent_norm).astype(jnp.bfloat16)
    scores = jnp.dot(unit_rows, cent_unit.T, preferred_element_type=jnp.float32)
    kernel = jnp.exp((scores - 1.0) * (2.0 / SIGMA_SCALE))
    first_resp = kernel / lax.optimization_barrier(jnp.sum(kernel, axis=1, keepdims=True))
    onehot = (batch[:, None] == jnp.arange(B)[None, :]).astype(jnp.float32)
    first_obs = jnp.dot(first_resp.T, onehot, precision=lax.Precision.HIGHEST)
    batch_sizes = lax.optimization_barrier(jnp.sum(onehot, axis=0))
    expect = lax.optimization_barrier(jnp.sum(first_obs, axis=1, keepdims=True)) * batch_sizes[None, :] / jnp.sum(batch_sizes)
    ratio = (expect + 1.0) / (first_obs + 1.0)
    penalty = ratio * ratio
    factor = jnp.dot(onehot, penalty.T, precision=lax.Precision.HIGHEST)
    weighted = kernel * factor
    response = (weighted / lax.optimization_barrier(jnp.sum(weighted, axis=1, keepdims=True))).astype(jnp.bfloat16)
    cent_sums = jnp.dot(response.T, unit_rows, preferred_element_type=jnp.float32)
    final_obs = jnp.dot(response.T, onehot.astype(jnp.bfloat16), preferred_element_type=jnp.float32)
    new_centroids = cent_sums / jnp.sqrt(lax.optimization_barrier(jnp.sum(cent_sums * cent_sums, axis=1, keepdims=True)) + EPSILON)
    return (smooth, new_centroids, final_obs)
```

```python
import functools

import jax
import jax.numpy as jnp
from jax import lax
from jax.experimental import pallas as pl
from jax.experimental.pallas import tpu as pltpu
from jax.sharding import PartitionSpec as P

B = 16
NBR = 30
DIFF_STEPS = 3
EPSILON = 1e-06
SIGMA_SCALE = 0.1
LANE = 128
MESH = pl.DeviceIdType.MESH
BF16 = jnp.bfloat16
F32 = jnp.float32


def padded(size, unit=LANE):
    return -(-size // unit) * unit


def split2(x):
    hi = x.astype(BF16)
    return hi, (x - hi.astype(F32)).astype(BF16)


def split3(x):
    hi = x.astype(BF16)
    rest = x - hi.astype(F32)
    mid = rest.astype(BF16)
    return hi, mid, (rest - mid.astype(F32)).astype(BF16)


def dot(a, b):
    return jnp.dot(a, b, preferred_element_type=F32)


def dot_nt(a, b):
    return lax.dot_general(a, b, (((1,), (1,)), ((), ())), preferred_element_type=F32)


def dot_tn(a, b):
    return lax.dot_general(a, b, (((0,), (0,)), ((), ())), preferred_element_type=F32)


def weights_kernel(rows, index_ref, weight_ref, hi_ref, lo_ref):
    wide = hi_ref.shape[1]
    hi_ref[...] = jnp.zeros_like(hi_ref)
    lo_ref[...] = jnp.zeros_like(lo_ref)
    tile = LANE
    for at in range(wide // tile):
        lanes = slice(at * tile, (at + 1) * tile)
        spans = ((0, at, wide // tile), (1, 0, wide // tile), (2, 0, at + 1))
        for block, first, last in spans:

            def fill(step, carry, block=block, lanes=lanes):
                start = pl.multiple_of(step * tile, tile)
                source = lax.broadcasted_iota(jnp.int32, (tile, tile), 0) + (
                    start + (block - 1) * rows
                )
                total = jnp.zeros((tile, tile), F32)
                for slot in range(NBR):
                    hit = index_ref[slot : slot + 1, lanes] == source
                    total += jnp.where(hit, weight_ref[slot : slot + 1, lanes], 0.0)
                inside = source < block * rows
                total = jnp.where(inside, total, 0.0)
                hi, lo = split2(total)
                hi_ref[pl.ds(block * wide + start, tile), lanes] = hi
                lo_ref[pl.ds(block * wide + start, tile), lanes] = lo
                return carry

            lax.fori_loop(first, last, fill, 0)


def main_kernel(
    dims,
    part_ref,
    w_hi,
    w_lo,
    inverse_ref,
    batch_ref,
    cent_ref,
    smooth_ref,
    new_cent_ref,
    obs_ref,
    rs_slots,
    state,
    halo,
    full,
    unit,
    k_hi,
    k_lo,
    fo_own,
    fo_in,
    fo_mid,
    fo_out,
    fo_all,
    pen3,
    cs,
    cs_in,
    cs_mid,
    cs_out,
    cs_end,
    fb_own,
    fb_in,
    fb_mid,
    fb_out,
    y_send,
    y_recv,
    h_send,
    h_recv,
    a_send,
    a_recv,
    c_send,
    c_recv,
):
    rows, k_real, n_gene, n_in, n_out = dims
    n_cell = n_in * n_out
    comps, wide = part_ref.shape
    share = comps // n_gene
    chunk = cent_ref.shape[0] // n_gene
    piece = chunk // n_in
    half = chunk // 2
    cell = lax.axis_index("cell")
    gene = lax.axis_index("gene")
    inner = lax.rem(cell, n_in)
    outer = lax.div(cell, n_in)
    core = lax.rem(cell, 2)

    def along_y(d):
        return (cell, lax.rem(gene + d, n_gene))

    def along_in(d):
        return (outer * n_in + lax.rem(inner + d, n_in), gene)

    def along_out(d):
        return (lax.rem(outer + d, n_out) * n_in + inner, gene)

    after = (lax.rem(cell + 1, n_cell), gene)
    before = (lax.rem(cell + n_cell - 1, n_cell), gene)
    twin = (cell + 1 - 2 * core, gene)

    barrier = pltpu.get_barrier_semaphore()
    greeted = (
        [along_y(d) for d in range(1, n_gene)]
        + [along_in(d) for d in range(1, n_in)]
        + [along_out(d) for d in range(1, n_out)]
        + [after, before]
    )
    for target in greeted:
        pl.semaphore_signal(barrier, inc=1, device_id=target, device_id_type=MESH)
    pl.semaphore_wait(barrier, len(greeted))

    pending = []

    def send(src, dst, send_sem, recv_sem, target):
        copy = pltpu.make_async_remote_copy(
            src_ref=src,
            dst_ref=dst,
            send_sem=send_sem,
            recv_sem=recv_sem,
            device_id=target,
            device_id_type=MESH,
        )
        copy.start()
        pending.append(copy)
        return copy

    copies = []
    for d in range(1, n_gene):
        to = lax.rem(gene + d, n_gene)
        copies.append(
            send(
                part_ref.at[pl.ds(pl.multiple_of(to * share, share), share)],
                rs_slots.at[d - 1],
                y_send.at[0, d - 1],
                y_recv.at[0, d - 1],
                along_y(d),
            )
        )
    own = pl.ds(pl.multiple_of(gene * share, share), share)
    value = part_ref[own, :]
    for d in range(1, n_gene):
        copies[d - 1].wait_recv()
        value += rs_slots[d - 1]

    def spread(field, block):
        hi, lo = split2(field)
        span = slice(block * wide, (block + 1) * wide)
        both = dot(jnp.concatenate([hi, lo], axis=0), w_hi[span, :])
        return both[:share] + both[share:] + dot(hi, w_lo[span, :])

    for step in range(DIFF_STEPS):
        state[step] = value
        up = send(
            state.at[step], halo.at[step, 0], h_send.at[step, 0], h_recv.at[step, 0], after
        )
        down = send(
            state.at[step], halo.at[step, 1], h_send.at[step, 1], h_recv.at[step, 1], before
        )
        total = value + spread(value, 1)
        up.wait_recv()
        total += spread(halo[step, 0], 0)
        down.wait_recv()
        total += spread(halo[step, 1], 2)
        value = total * inverse_ref[0:1, :]

    full[own, :] = value
    copies = []
    for d in range(1, n_gene):
        copies.append(
            send(full.at[own], full.at[own], y_send.at[1, d - 1], y_recv.at[1, d - 1], along_y(d))
        )
    smooth_ref[...] = value[:, :rows]
    onehot = (
        batch_ref[0:1, :] == lax.broadcasted_iota(jnp.int32, (B, wide), 0)
    ).astype(F32)
    counts = jnp.sum(onehot, axis=1, keepdims=True)
    hot = onehot.astype(BF16)
    for copy in copies:
        copy.wait_recv()

    whole = full[...]
    norm = jnp.sqrt(jnp.sum(whole * whole, axis=0, keepdims=True) + EPSILON)
    unit[...] = (whole / norm).astype(BF16)

    def kernel_rows(start):
        scores = dot(cent_ref[pl.ds(start, chunk), :], unit[...])
        number = lax.broadcasted_iota(jnp.int32, (chunk, wide), 0) + start
        return jnp.where(number < k_real, jnp.exp((scores - 1.0) * (2.0 / SIGMA_SCALE)), 0.0)

    def first(at, sums):
        start = pl.multiple_of(at * chunk, chunk)
        values = kernel_rows(start)
        hi, lo = split2(values)
        k_hi[pl.ds(start, chunk), :] = hi
        k_lo[pl.ds(start, chunk), :] = lo
        return sums + jnp.sum(values, axis=0, keepdims=True)

    sums = lax.fori_loop(0, n_gene, first, jnp.zeros((1, wide), F32))
    mine = pl.multiple_of(gene * chunk, chunk)
    kernel_own = kernel_rows(mine)
    hi, lo = split2(kernel_own / sums)
    observed = dot_nt(hot, hi) + dot_nt(hot, lo)
    column = lax.broadcasted_iota(jnp.int32, (B, chunk), 1) + gene * chunk
    fo_own[...] = jnp.where(column == n_gene * chunk - 1, counts, observed)

    def all_sum(source, slots, target_of, count, sems, at):
        send_sem, recv_sem = sems
        copies = []
        for d in range(1, count):
            copies.append(
                send(
                    source,
                    slots.at[d - 1],
                    send_sem.at[at, d - 1],
                    recv_sem.at[at, d - 1],
                    target_of(d),
                )
            )

        def finish():
            total = source[...]
            for d in range(1, count):
                copies[d - 1].wait_recv()
                total += slots[d - 1]
            return total

        return finish

    a_sems = (a_send, a_recv)
    fo_mid[...] = all_sum(fo_own, fo_in, along_in, n_in, a_sems, 0)()
    fo_all[gene] = all_sum(fo_mid, fo_out, along_out, n_out, a_sems, 1)()
    copies = []
    for d in range(1, n_gene):
        copies.append(
            send(
                fo_all.at[gene],
                fo_all.at[gene],
                y_send.at[2, d - 1],
                y_recv.at[2, d - 1],
                along_y(d),
            )
        )
    for copy in copies:
        copy.wait_recv()

    sizes = fo_all[n_gene - 1][:, chunk - 1 : chunk]
    portion = sizes / jnp.sum(sizes, axis=0, keepdims=True)

    def penalty_of(seen):
        ratio = (jnp.sum(seen, axis=0, keepdims=True) * portion + 1.0) / (seen + 1.0)
        return jnp.concatenate(split3(ratio * ratio), axis=0)

    for at in range(n_gene):
        pen3[:, at * chunk : (at + 1) * chunk] = penalty_of(fo_all[at])
    parts = dot(pen3[...], k_hi[...]) + dot(pen3[...], k_lo[...])
    parts = (parts[:B] + parts[B : 2 * B]) + parts[2 * B :]
    weighted = jnp.sum(parts * onehot, axis=0, keepdims=True)
    lane = lax.broadcasted_iota(jnp.int32, (1, wide), 1)
    weighted = jnp.where(lane < rows, weighted, 1.0)
    factor = dot_tn(penalty_of(fo_all[gene]), jnp.concatenate([hot, hot, hot], axis=0))
    response = (kernel_own * factor / weighted).astype(BF16)
    cs[...] = dot_nt(response, unit[...])
    fb_own[...] = dot_nt(hot, response)

    c_copies = []
    for d in range(1, n_in):
        to = lax.rem(inner + d, n_in)
        c_copies.append(
            send(
                cs.at[pl.ds(pl.multiple_of(to * piece, piece), piece)],
                cs_in.at[d - 1],
                c_send.at[0, d - 1],
                c_recv.at[0, d - 1],
                along_in(d),
            )
        )
    fb_first = all_sum(fb_own, fb_in, along_in, n_in, a_sems, 2)
    piece_sum = cs[pl.ds(pl.multiple_of(inner * piece, piece), piece), :]
    for d in range(1, n_in):
        c_copies[d - 1].wait_recv()
        piece_sum += cs_in[d - 1]
    cs_mid[...] = piece_sum
    cs_second = all_sum(cs_mid, cs_out, along_out, n_out, (c_send, c_recv), 1)
    fb_mid[...] = fb_first()
    fb_second = all_sum(fb_mid, fb_out, along_out, n_out, a_sems, 3)
    piece_sum = cs_second()
    length = jnp.sqrt(jnp.sum(piece_sum * piece_sum, axis=1, keepdims=True) + EPSILON)
    cs_end[...] = piece_sum / length

    here = pl.ds(pl.multiple_of(gene * chunk + inner * piece, piece), piece)
    copies = []
    for d in range(1, n_in):
        copies.append(
            send(
                cs_end,
                new_cent_ref.at[here],
                c_send.at[2, d - 1],
                c_recv.at[2, d - 1],
                along_in(d),
            )
        )
    new_cent_ref[here, :] = cs_end[...]
    obs_ref[gene] = fb_second()
    obs_copies = []
    for d in range(1, n_gene):
        obs_copies.append(
            send(
                obs_ref.at[gene],
                obs_ref.at[gene],
                y_send.at[3, d - 1],
                y_recv.at[3, d - 1],
                along_y(d),
            )
        )
    for copy in copies:
        copy.wait_recv()

    def half_of(number):
        return pl.ds(pl.multiple_of(number * chunk + core * half, half), half)

    copies = []
    for d in range(1, n_gene):
        copies.append(
            send(
                new_cent_ref.at[half_of(gene)],
                new_cent_ref.at[half_of(gene)],
                y_send.at[4, d - 1],
                y_recv.at[4, d - 1],
                along_y(d),
            )
        )
    shared = []
    for d in range(1, n_gene):
        copies[d - 1].wait_recv()
        rows_at = half_of(lax.rem(gene + n_gene - d, n_gene))
        shared.append(
            send(
                new_cent_ref.at[rows_at],
                new_cent_ref.at[rows_at],
                y_send.at[5, d - 1],
                y_recv.at[5, d - 1],
                twin,
            )
        )
    for copy in obs_copies:
        copy.wait_recv()
    for copy in shared:
        copy.wait_recv()
    for copy in pending:
        copy.wait_send()


def shards(n_in, expression, gene_mean, loadings, nbr_index, nbr_count, nbr_weight, batch, centroids):
    rows = expression.shape[0]
    comps = loadings.shape[1]
    k_real = centroids.shape[0]
    n_gene = lax.axis_size("gene")
    n_out = lax.axis_size("cell") // n_in
    wide = padded(rows)
    k_wide = padded(k_real)
    share = comps // n_gene
    chunk = k_wide // n_gene
    piece = chunk // n_in
    lanes = ((0, 0), (0, wide - rows))

    mean_proj = jnp.dot(gene_mean, loadings.astype(F32), precision=lax.Precision.HIGHEST)
    partial = lax.dot_general(
        loadings, expression, (((0,), (1,)), ((), ())), preferred_element_type=F32
    )
    partial = jnp.pad(partial - mean_proj[:, None], lanes)

    live = jnp.arange(NBR)[:, None] < nbr_count[None, :]
    weights = jnp.where(live, nbr_weight.T, jnp.float32(0.0))
    inverse = 1.0 / (1.0 + jnp.sum(weights, axis=0, keepdims=True))
    inverse = jnp.pad(jnp.broadcast_to(inverse, (8, rows)), lanes)
    local = nbr_index.T - lax.axis_index("cell") * rows
    slots = ((0, 32 - NBR), (0, wide - rows))
    local = jnp.pad(local, slots)
    weights = jnp.pad(weights, slots)
    batch_row = jnp.pad(jnp.broadcast_to(batch[None, :], (8, rows)), lanes, constant_values=-1)
    cent_norm = jnp.sqrt(jnp.sum(centroids * centroids, axis=1, keepdims=True) + EPSILON)
    cent_unit = jnp.pad((centroids / cent_norm).astype(BF16), ((0, k_wide - k_real), (0, 0)))

    vmem = pl.BlockSpec(memory_space=pltpu.VMEM)
    w_hi, w_lo = pl.pallas_call(
        functools.partial(weights_kernel, rows),
        out_shape=[jax.ShapeDtypeStruct((3 * wide, wide), BF16)] * 2,
        in_specs=[vmem] * 2,
        out_specs=[vmem] * 2,
        compiler_params=pltpu.CompilerParams(vmem_limit_bytes=32 * 1024 * 1024),
    )(local, weights)

    dims = (rows, k_real, n_gene, n_in, n_out)
    dma = pltpu.SemaphoreType.DMA
    smooth, new_cent, obs = pl.pallas_call(
        functools.partial(main_kernel, dims),
        out_shape=[
            jax.ShapeDtypeStruct((share, rows), F32),
            jax.ShapeDtypeStruct((k_wide, comps), F32),
            jax.ShapeDtypeStruct((n_gene, B, chunk), F32),
        ],
        in_specs=[vmem] * 6,
        out_specs=[vmem] * 3,
        scratch_shapes=[
            pltpu.VMEM((n_gene - 1, share, wide), F32),
            pltpu.VMEM((DIFF_STEPS, share, wide), F32),
            pltpu.VMEM((DIFF_STEPS, 2, share, wide), F32),
            pltpu.VMEM((comps, wide), F32),
            pltpu.VMEM((comps, wide), BF16),
            pltpu.VMEM((k_wide, wide), BF16),
            pltpu.VMEM((k_wide, wide), BF16),
            pltpu.VMEM((B, chunk), F32),
            pltpu.VMEM((n_in - 1, B, chunk), F32),
            pltpu.VMEM((B, chunk), F32),
            pltpu.VMEM((n_out - 1, B, chunk), F32),
            pltpu.VMEM((n_gene, B, chunk), F32),
            pltpu.VMEM((3 * B, k_wide), BF16),
            pltpu.VMEM((chunk, comps), F32),
            pltpu.VMEM((n_in - 1, piece, comps), F32),
            pltpu.VMEM((piece, comps), F32),
            pltpu.VMEM((n_out - 1, piece, comps), F32),
            pltpu.VMEM((piece, comps), F32),
            pltpu.VMEM((B, chunk), F32),
            pltpu.VMEM((n_in - 1, B, chunk), F32),
            pltpu.VMEM((B, chunk), F32),
            pltpu.VMEM((n_out - 1, B, chunk), F32),
            dma((6, n_gene - 1)),
            dma((6, n_gene - 1)),
            dma((DIFF_STEPS, 2)),
            dma((DIFF_STEPS, 2)),
            dma((4, max(n_in, n_out) - 1)),
            dma((4, max(n_in, n_out) - 1)),
            dma((3, max(n_in, n_out) - 1)),
            dma((3, max(n_in, n_out) - 1)),
        ],
        compiler_params=pltpu.CompilerParams(
            collective_id=0, has_side_effects=True, vmem_limit_bytes=48 * 1024 * 1024
        ),
    )(partial, w_hi, w_lo, inverse, batch_row, cent_unit)

    final_obs = obs.transpose(0, 2, 1).reshape(k_wide, B)[:k_real]
    return (smooth.T, new_cent[:k_real], final_obs)


def solution(mesh):
    in_specs = (
        P("cell", "gene"),
        P("gene"),
        P("gene", None),
        P("cell", None),
        P("cell"),
        P("cell", None),
        P("cell"),
        P(),
    )
    out_specs = (P("cell", "gene"), P(), P())
    n_in = 8 if mesh.shape["cell"] % 64 == 0 else 2
    body = functools.partial(shards, n_in)
    return jax.shard_map(body, mesh=mesh, in_specs=in_specs, out_specs=out_specs, check_vma=False)
```

```python
import functools

import jax
import jax.numpy as jnp
from jax import lax
from jax.experimental import pallas as pl
from jax.experimental.pallas import tpu as pltpu
from jax.sharding import PartitionSpec as P

B = 16
NBR = 30
DIFF_STEPS = 3
EPSILON = 1e-06
SIGMA_SCALE = 0.1
LANE = 128
MESH = pl.DeviceIdType.MESH
BF16 = jnp.bfloat16
F32 = jnp.float32


def padded(size, unit=LANE):
    return -(-size // unit) * unit


def split2(x):
    hi = x.astype(BF16)
    return hi, (x - hi.astype(F32)).astype(BF16)


def split3(x):
    hi = x.astype(BF16)
    rest = x - hi.astype(F32)
    mid = rest.astype(BF16)
    return hi, mid, (rest - mid.astype(F32)).astype(BF16)


def dot(a, b):
    return jnp.dot(a, b, preferred_element_type=F32)


def dot_nt(a, b):
    return lax.dot_general(a, b, (((1,), (1,)), ((), ())), preferred_element_type=F32)


def dot_tn(a, b):
    return lax.dot_general(a, b, (((0,), (0,)), ((), ())), preferred_element_type=F32)


def farthest_first(count):
    return sorted(range(1, count), key=lambda d: -min(d, count - d))


def build_weights(rows, index_ref, weight_ref, hi_ref, lo_ref):
    wide = hi_ref.shape[1]
    hi_ref[...] = jnp.zeros_like(hi_ref)
    lo_ref[...] = jnp.zeros_like(lo_ref)
    tile = LANE
    for at in range(wide // tile):
        lanes = slice(at * tile, (at + 1) * tile)
        spans = ((0, at, wide // tile), (1, 0, wide // tile), (2, 0, at + 1))
        for block, first, last in spans:

            def fill(step, carry, block=block, lanes=lanes):
                start = pl.multiple_of(step * tile, tile)
                source = lax.broadcasted_iota(jnp.int32, (tile, tile), 0) + (
                    start + (block - 1) * rows
                )
                total = jnp.zeros((tile, tile), F32)
                for slot in range(NBR):
                    hit = index_ref[slot : slot + 1, lanes] == source
                    total += jnp.where(hit, weight_ref[slot : slot + 1, lanes], 0.0)
                total = jnp.where(source < block * rows, total, 0.0)
                hi, lo = split2(total)
                hi_ref[pl.ds(block * wide + start, tile), lanes] = hi
                lo_ref[pl.ds(block * wide + start, tile), lanes] = lo
                return carry

            lax.fori_loop(first, last, fill, 0)


def main_kernel(
    dims,
    expr_hbm,
    mean_ref,
    load_hbm,
    index_hbm,
    count_ref,
    weight_hbm,
    batch_ref,
    centroid_hbm,
    smooth_ref,
    cent_out,
    obs_out,
    new_cent_ref,
    obs_ref,
    expr_ref,
    load_ref,
    index_ref,
    weight_ref,
    centroid_ref,
    l_sem,
    part_ref,
    idx,
    wgt,
    w_hi,
    w_lo,
    cent_ref,
    rs_slots,
    state,
    halo,
    full,
    unit,
    k_hi,
    k_lo,
    fo_own,
    fo_in,
    fo_mid,
    fo_out,
    fo_all,
    pen3,
    cs,
    cs_in,
    cs_mid,
    cs_out,
    fb_own,
    fb_in,
    fb_mid,
    fb_out,
    y_send,
    y_recv,
    h_send,
    h_recv,
    a_send,
    a_recv,
    c_send,
    c_recv,
    t_send,
    t_recv,
):
    rows, k_real, n_gene, n_in, n_out = dims
    n_cell = n_in * n_out
    comps, wide = part_ref.shape
    y_order, in_order = farthest_first(n_gene), farthest_first(n_in)
    share = comps // n_gene
    chunk = cent_ref.shape[0] // n_gene
    piece = chunk // n_in
    n_x = n_in // 2
    cell = lax.axis_index("cell")
    gene = lax.axis_index("gene")
    inner = lax.rem(cell, n_in)
    outer = lax.div(cell, n_in)
    core = lax.rem(cell, 2)

    def along_y(d):
        return (cell, lax.rem(gene + d, n_gene))

    def along_in(d):
        return (outer * n_in + lax.rem(inner + d, n_in), gene)

    def along_out(d):
        return (lax.rem(outer + d, n_out) * n_in + inner, gene)

    after = (lax.rem(cell + 1, n_cell), gene)
    before = (lax.rem(cell + n_cell - 1, n_cell), gene)
    twin = (cell + 1 - 2 * core, gene)

    brought = [
        pltpu.make_async_copy(source, target, l_sem.at[at])
        for at, (source, target) in enumerate(
            (
                (load_hbm, load_ref),
                (expr_hbm, expr_ref),
                (index_hbm, index_ref),
                (weight_hbm, weight_ref),
                (centroid_hbm, centroid_ref),
            )
        )
    ]
    for copy in brought:
        copy.start()

    barrier = pltpu.get_barrier_semaphore()
    greeted = (
        [along_y(d) for d in range(1, n_gene)]
        + [along_in(d) for d in range(1, n_in)]
        + [along_out(d) for d in range(1, n_out)]
        + [after, before]
    )
    for target in greeted:
        pl.semaphore_signal(barrier, inc=1, device_id=target, device_id_type=MESH)

    mean = jnp.concatenate(
        [m.astype(F32) for m in split3(mean_ref[...][None, :])] + [jnp.zeros((5, mean_ref.shape[0]), F32)],
        axis=0,
    ).astype(BF16)
    brought[0].wait()
    turned = load_ref[...].T
    offset = jnp.sum(dot_nt(turned, mean), axis=1, keepdims=True)
    brought[1].wait()
    part_ref[:, rows:] = jnp.zeros((comps, wide - rows), F32)
    part_ref[:, :rows] = dot_nt(turned, expr_ref[...]) - offset
    pl.semaphore_wait(barrier, len(greeted))

    pending = []

    def send(src, dst, send_sem, recv_sem, target):
        copy = pltpu.make_async_remote_copy(
            src_ref=src,
            dst_ref=dst,
            send_sem=send_sem,
            recv_sem=recv_sem,
            device_id=target,
            device_id_type=MESH,
        )
        copy.start()
        pending.append(copy)
        return copy

    copies = []
    for d in y_order:
        to = lax.rem(gene + d, n_gene)
        copies.append(
            send(
                part_ref.at[pl.ds(pl.multiple_of(to * share, share), share)],
                rs_slots.at[d - 1],
                y_send.at[0, d - 1],
                y_recv.at[0, d - 1],
                along_y(d),
            )
        )
    own = pl.ds(pl.multiple_of(gene * share, share), share)

    brought[2].wait()
    brought[3].wait()
    idx[...] = jnp.full(idx.shape, -(4 * rows), jnp.int32)
    idx[:NBR, :rows] = index_ref[...] - cell * rows
    live = lax.broadcasted_iota(jnp.int32, (NBR, rows), 0) < count_ref[...][None, :]
    kept = jnp.where(live, weight_ref[...], 0.0)
    wgt[...] = jnp.zeros_like(wgt)
    wgt[:NBR, :rows] = kept
    build_weights(rows, idx, wgt, w_hi, w_lo)
    inverse = 1.0 / (1.0 + jnp.sum(wgt[...], axis=0, keepdims=True))
    brought[4].wait()
    cents = centroid_ref[...]
    cent_norm = jnp.sqrt(jnp.sum(cents * cents, axis=1, keepdims=True) + EPSILON)
    cent_ref[...] = jnp.concatenate(
        [cents / cent_norm, jnp.zeros((n_gene * chunk - k_real, comps), F32)], axis=0
    ).astype(BF16)
    onehot = jnp.concatenate(
        [
            (batch_ref[...][None, :] == lax.broadcasted_iota(jnp.int32, (B, rows), 0)).astype(F32),
            jnp.zeros((B, wide - rows), F32),
        ],
        axis=1,
    )
    counts = jnp.sum(onehot, axis=1, keepdims=True)
    hot = onehot.astype(BF16)

    value = part_ref[own, :]
    for d, copy in zip(y_order, copies):
        copy.wait_recv()
        value += rs_slots[d - 1]

    def spread(field, block):
        hi, lo = split2(field)
        span = slice(block * wide, (block + 1) * wide)
        both = dot(jnp.concatenate([hi, lo], axis=0), w_hi[span, :])
        return both[:share] + both[share:] + dot(hi, w_lo[span, :])

    for step in range(DIFF_STEPS):
        state[step] = value
        up = send(
            state.at[step], halo.at[step, 0], h_send.at[step, 0], h_recv.at[step, 0], after
        )
        down = send(
            state.at[step], halo.at[step, 1], h_send.at[step, 1], h_recv.at[step, 1], before
        )
        total = value + spread(value, 1)
        up.wait_recv()
        total += spread(halo[step, 0], 0)
        down.wait_recv()
        total += spread(halo[step, 1], 2)
        value = total * inverse

    full[own, :] = value
    copies = []
    for d in y_order:
        copies.append(
            send(full.at[own], full.at[own], y_send.at[1, d - 1], y_recv.at[1, d - 1], along_y(d))
        )
    smooth_ref[...] = value[:, :rows]
    for copy in copies:
        copy.wait_recv()

    whole = full[...]
    norm = jnp.sqrt(jnp.sum(whole * whole, axis=0, keepdims=True) + EPSILON)
    unit[...] = (whole / norm).astype(BF16)

    def kernel_rows(start):
        scores = dot(cent_ref[pl.ds(start, chunk), :], unit[...])
        number = lax.broadcasted_iota(jnp.int32, (chunk, wide), 0) + start
        return jnp.where(number < k_real, jnp.exp((scores - 1.0) * (2.0 / SIGMA_SCALE)), 0.0)

    def first(at, sums):
        start = pl.multiple_of(at * chunk, chunk)
        values = kernel_rows(start)
        hi, lo = split2(values)
        k_hi[pl.ds(start, chunk), :] = hi
        k_lo[pl.ds(start, chunk), :] = lo
        return sums + jnp.sum(values, axis=0, keepdims=True)

    sums = lax.fori_loop(0, n_gene, first, jnp.zeros((1, wide), F32))
    mine = pl.multiple_of(gene * chunk, chunk)
    kernel_own = kernel_rows(mine)
    hi, lo = split2(kernel_own / sums)
    observed = dot_nt(hot, hi) + dot_nt(hot, lo)
    column = lax.broadcasted_iota(jnp.int32, (B, chunk), 1) + gene * chunk
    fo_own[...] = jnp.where(column == n_gene * chunk - 1, counts, observed)

    def all_sum(source, slots, target_of, count, sems, at):
        send_sem, recv_sem = sems
        copies = []
        for d in farthest_first(count):
            copies.append(
                send(
                    source,
                    slots.at[d - 1],
                    send_sem.at[at, d - 1],
                    recv_sem.at[at, d - 1],
                    target_of(d),
                )
            )

        def finish():
            total = source[...]
            for d, copy in zip(farthest_first(count), copies):
                copy.wait_recv()
                total += slots[d - 1]
            return total

        return finish

    a_sems = (a_send, a_recv)
    fo_mid[...] = all_sum(fo_own, fo_in, along_in, n_in, a_sems, 0)()
    fo_all[gene] = all_sum(fo_mid, fo_out, along_out, n_out, a_sems, 1)()
    copies = []
    for d in y_order:
        copies.append(
            send(
                fo_all.at[gene],
                fo_all.at[gene],
                y_send.at[2, d - 1],
                y_recv.at[2, d - 1],
                along_y(d),
            )
        )
    for copy in copies:
        copy.wait_recv()

    sizes = fo_all[n_gene - 1][:, chunk - 1 : chunk]
    portion = sizes / jnp.sum(sizes, axis=0, keepdims=True)

    def penalty_of(seen):
        ratio = (jnp.sum(seen, axis=0, keepdims=True) * portion + 1.0) / (seen + 1.0)
        return jnp.concatenate(split3(ratio * ratio), axis=0)

    for at in range(n_gene):
        pen3[:, at * chunk : (at + 1) * chunk] = penalty_of(fo_all[at])
    parts = dot(pen3[...], k_hi[...]) + dot(pen3[...], k_lo[...])
    parts = (parts[:B] + parts[B : 2 * B]) + parts[2 * B :]
    weighted = jnp.sum(parts * onehot, axis=0, keepdims=True)
    lane = lax.broadcasted_iota(jnp.int32, (1, wide), 1)
    weighted = jnp.where(lane < rows, weighted, 1.0)
    factor = dot_tn(penalty_of(fo_all[gene]), jnp.concatenate([hot, hot, hot], axis=0))
    response = (kernel_own * factor / weighted).astype(BF16)
    cs[...] = dot_nt(response, unit[...])
    fb_own[...] = dot_nt(hot, response)

    c_copies = []
    for d in in_order:
        to = lax.rem(inner + d, n_in)
        c_copies.append(
            send(
                cs.at[pl.ds(pl.multiple_of(to * piece, piece), piece)],
                cs_in.at[d - 1],
                c_send.at[0, d - 1],
                c_recv.at[0, d - 1],
                along_in(d),
            )
        )
    fb_first = all_sum(fb_own, fb_in, along_in, n_in, a_sems, 2)
    piece_sum = cs[pl.ds(pl.multiple_of(inner * piece, piece), piece), :]
    for d, copy in zip(in_order, c_copies):
        copy.wait_recv()
        piece_sum += cs_in[d - 1]
    cs_mid[...] = piece_sum
    cs_second = all_sum(cs_mid, cs_out, along_out, n_out, (c_send, c_recv), 1)
    fb_mid[...] = fb_first()
    fb_second = all_sum(fb_mid, fb_out, along_out, n_out, a_sems, 3)
    piece_sum = cs_second()
    length = jnp.sqrt(jnp.sum(piece_sum * piece_sum, axis=1, keepdims=True) + EPSILON)

    new_cent_ref[gene, inner] = piece_sum / length
    copies = []
    for d in y_order:
        copies.append(
            send(
                new_cent_ref.at[gene, inner],
                new_cent_ref.at[gene, inner],
                y_send.at[4, d - 1],
                y_recv.at[4, d - 1],
                along_y(d),
            )
        )
    obs_ref[gene] = fb_second()
    obs_copies = []
    for d in y_order:
        obs_copies.append(
            send(
                obs_ref.at[gene],
                obs_ref.at[gene],
                y_send.at[3, d - 1],
                y_recv.at[3, d - 1],
                along_y(d),
            )
        )
    for copy in copies:
        copy.wait_recv()

    def column(number, target, sems, at):
        send_sem, recv_sem = sems
        return send(
            new_cent_ref.at[:, number],
            new_cent_ref.at[:, number],
            send_sem.at[at],
            recv_sem.at[at],
            target,
        )

    x_order = farthest_first(n_x)
    copies = [column(inner, along_in(2 * e), (c_send.at[2], c_recv.at[2]), e) for e in x_order]
    shared = [column(inner, twin, (t_send, t_recv), 0)]
    for e, copy in zip(x_order, copies):
        copy.wait_recv()
        number = lax.rem(inner + n_in - 2 * e, n_in)
        shared.append(column(number, twin, (t_send, t_recv), e))
    for copy in obs_copies:
        copy.wait_recv()
    for at in range(n_gene):
        size = min(chunk, k_real - at * chunk)
        obs_out[:, at * chunk : at * chunk + size] = obs_ref[at][:, :size]
    for copy in shared:
        copy.wait_recv()
    for at in range(n_gene):
        for part in range(n_in):
            start = at * chunk + part * piece
            size = min(piece, k_real - start)
            if size > 0:
                cent_out[start : start + size, :] = new_cent_ref[at, part][:size]
    for copy in pending:
        copy.wait_send()


def shards(n_in, expression, gene_mean, loadings, nbr_index, nbr_count, nbr_weight, batch, centroids):
    rows = expression.shape[0]
    comps = loadings.shape[1]
    k_real = centroids.shape[0]
    n_gene = lax.axis_size("gene")
    n_out = lax.axis_size("cell") // n_in
    wide = padded(rows)
    k_wide = padded(k_real)
    share = comps // n_gene
    chunk = k_wide // n_gene
    piece = chunk // n_in
    vmem = pl.BlockSpec(memory_space=pltpu.VMEM)
    hbm = pl.BlockSpec(memory_space=pltpu.HBM)
    dims = (rows, k_real, n_gene, n_in, n_out)
    dma = pltpu.SemaphoreType.DMA
    smooth, new_cent, obs = pl.pallas_call(
        functools.partial(main_kernel, dims),
        out_shape=[
            jax.ShapeDtypeStruct((share, rows), F32),
            jax.ShapeDtypeStruct((k_real, comps), F32),
            jax.ShapeDtypeStruct((B, k_real), F32),
        ],
        in_specs=[hbm, vmem, hbm, hbm, vmem, hbm, vmem, hbm],
        out_specs=[vmem] * 3,
        scratch_shapes=[
            pltpu.VMEM((n_gene, n_in, piece, comps), F32),
            pltpu.VMEM((n_gene, B, chunk), F32),
            pltpu.VMEM(expression.shape, BF16),
            pltpu.VMEM(loadings.shape, BF16),
            pltpu.VMEM((NBR, rows), jnp.int32),
            pltpu.VMEM((NBR, rows), F32),
            pltpu.VMEM(centroids.shape, F32),
            dma((5,)),
            pltpu.VMEM((comps, wide), F32),
            pltpu.VMEM((32, wide), jnp.int32),
            pltpu.VMEM((32, wide), F32),
            pltpu.VMEM((3 * wide, wide), BF16),
            pltpu.VMEM((3 * wide, wide), BF16),
            pltpu.VMEM((k_wide, comps), BF16),
            pltpu.VMEM((n_gene - 1, share, wide), F32),
            pltpu.VMEM((DIFF_STEPS, share, wide), F32),
            pltpu.VMEM((DIFF_STEPS, 2, share, wide), F32),
            pltpu.VMEM((comps, wide), F32),
            pltpu.VMEM((comps, wide), BF16),
            pltpu.VMEM((k_wide, wide), BF16),
            pltpu.VMEM((k_wide, wide), BF16),
            pltpu.VMEM((B, chunk), F32),
            pltpu.VMEM((n_in - 1, B, chunk), F32),
            pltpu.VMEM((B, chunk), F32),
            pltpu.VMEM((n_out - 1, B, chunk), F32),
            pltpu.VMEM((n_gene, B, chunk), F32),
            pltpu.VMEM((3 * B, k_wide), BF16),
            pltpu.VMEM((chunk, comps), F32),
            pltpu.VMEM((n_in - 1, piece, comps), F32),
            pltpu.VMEM((piece, comps), F32),
            pltpu.VMEM((n_out - 1, piece, comps), F32),
            pltpu.VMEM((B, chunk), F32),
            pltpu.VMEM((n_in - 1, B, chunk), F32),
            pltpu.VMEM((B, chunk), F32),
            pltpu.VMEM((n_out - 1, B, chunk), F32),
            dma((6, n_gene - 1)),
            dma((6, n_gene - 1)),
            dma((DIFF_STEPS, 2)),
            dma((DIFF_STEPS, 2)),
            dma((4, max(n_in, n_out) - 1)),
            dma((4, max(n_in, n_out) - 1)),
            dma((3, max(n_in, n_out) - 1)),
            dma((3, max(n_in, n_out) - 1)),
            dma((n_in // 2,)),
            dma((n_in // 2,)),
        ],
        compiler_params=pltpu.CompilerParams(
            collective_id=0, has_side_effects=True, vmem_limit_bytes=60 * 1024 * 1024
        ),
    )(
        expression,
        gene_mean,
        loadings,
        nbr_index.T,
        nbr_count,
        nbr_weight.T,
        batch,
        centroids,
    )

    return (smooth.T, new_cent, obs.T)


def solution(mesh):
    in_specs = (
        P("cell", "gene"),
        P("gene"),
        P("gene", None),
        P("cell", None),
        P("cell"),
        P("cell", None),
        P("cell"),
        P(),
    )
    out_specs = (P("cell", "gene"), P(), P())
    n_in = 8 if mesh.shape["cell"] % 64 == 0 else 4
    body = functools.partial(shards, n_in)
    return jax.shard_map(body, mesh=mesh, in_specs=in_specs, out_specs=out_specs, check_vma=False)
```

```python
import functools

import jax
import jax.numpy as jnp
from jax import lax
from jax.experimental import pallas as pl
from jax.experimental.pallas import tpu as pltpu
from jax.sharding import PartitionSpec as P

B = 16
NBR = 30
DIFF_STEPS = 3
EPSILON = 1e-06
SIGMA_SCALE = 0.1
LANE = 128
MESH = pl.DeviceIdType.MESH
BF16 = jnp.bfloat16
F32 = jnp.float32


def padded(size, unit=LANE):
    return -(-size // unit) * unit


def split2(x):
    hi = x.astype(BF16)
    return hi, (x - hi.astype(F32)).astype(BF16)


def split3(x):
    hi = x.astype(BF16)
    rest = x - hi.astype(F32)
    mid = rest.astype(BF16)
    return hi, mid, (rest - mid.astype(F32)).astype(BF16)


def dot(a, b):
    return jnp.dot(a, b, preferred_element_type=F32)


def dot_nt(a, b):
    return lax.dot_general(a, b, (((1,), (1,)), ((), ())), preferred_element_type=F32)


def dot_tn(a, b):
    return lax.dot_general(a, b, (((0,), (0,)), ((), ())), preferred_element_type=F32)


def farthest_first(count):
    return sorted(range(1, count), key=lambda d: -min(d, count - d))


def build_weights(rows, block, index_ref, weight_ref, hi_ref, lo_ref):
    wide = hi_ref.shape[1]
    tile = LANE
    tiles = wide // tile
    base = block * wide
    span = slice(base, base + wide)
    hi_ref[span, :] = jnp.zeros((wide, wide), BF16)
    lo_ref[span, :] = jnp.zeros((wide, wide), BF16)
    for at in range(tiles):
        lanes = slice(at * tile, (at + 1) * tile)
        first, last = ((at, tiles), (0, tiles), (0, at + 1))[block]

        def rows_of(start, height, lanes=lanes):
            source = lax.broadcasted_iota(jnp.int32, (height, tile), 0) + (
                start + (block - 1) * rows
            )
            total = jnp.zeros((height, tile), F32)
            for slot in range(NBR):
                hit = index_ref[slot : slot + 1, lanes] == source
                total += jnp.where(hit, weight_ref[slot : slot + 1, lanes], 0.0)
            hi, lo = split2(total)
            hi_ref[pl.ds(base + start, height), lanes] = hi
            lo_ref[pl.ds(base + start, height), lanes] = lo

        def fill(step, carry, rows_of=rows_of):
            rows_of(pl.multiple_of(step * tile, tile), tile)
            return carry

        lax.fori_loop(first, min(last, rows // tile), fill, 0)
        if last == tiles and rows % tile:
            rows_of(rows // tile * tile, rows % tile)


def main_kernel(
    dims,
    expr_hbm,
    mean_ref,
    load_hbm,
    index_hbm,
    count_ref,
    weight_hbm,
    batch_ref,
    centroid_hbm,
    smooth_ref,
    cent_out,
    obs_out,
    new_cent_ref,
    obs_ref,
    expr_ref,
    load_ref,
    index_ref,
    weight_ref,
    centroid_ref,
    l_sem,
    part_ref,
    idx,
    wgt,
    w_hi,
    w_lo,
    cent_ref,
    rs_slots,
    state,
    halo,
    full,
    unit,
    k_hi,
    k_lo,
    fo_own,
    fo_in,
    fo_mid,
    fo_out,
    fo_all,
    pen3,
    cs,
    cs_in,
    cs_mid,
    cs_out,
    fb_own,
    fb_in,
    fb_mid,
    fb_out,
    y_send,
    y_recv,
    h_send,
    h_recv,
    a_send,
    a_recv,
    c_send,
    c_recv,
    t_send,
    t_recv,
    x_send,
    x_recv,
    o_sem,
    turn,
    smooth_v,
    obs_v,
):
    rows, k_real, n_gene, n_in, n_out = dims
    n_cell = n_in * n_out
    comps, wide = part_ref.shape
    y_order, in_order = farthest_first(n_gene), farthest_first(n_in)
    share = comps // n_gene
    chunk = cent_ref.shape[0] // n_gene
    piece = chunk // n_in
    n_x = n_in // 2
    cell = lax.axis_index("cell")
    gene = lax.axis_index("gene")
    inner = lax.rem(cell, n_in)
    outer = lax.div(cell, n_in)
    core = lax.rem(cell, 2)

    def along_y(d):
        return (cell, lax.rem(gene + d, n_gene))

    def along_in(d):
        return (outer * n_in + lax.rem(inner + d, n_in), gene)

    def along_out(d):
        return (lax.rem(outer + d, n_out) * n_in + inner, gene)

    after = (lax.rem(cell + 1, n_cell), gene)
    before = (lax.rem(cell + n_cell - 1, n_cell), gene)
    twin = (cell + 1 - 2 * core, gene)

    brought = [
        pltpu.make_async_copy(source, target, l_sem.at[at])
        for at, (source, target) in enumerate(
            (
                (load_hbm, load_ref),
                (expr_hbm, expr_ref),
                (index_hbm, index_ref),
                (weight_hbm, weight_ref),
                (centroid_hbm, centroid_ref),
            )
        )
    ]
    for copy in brought:
        copy.start()

    barrier = pltpu.get_barrier_semaphore()
    greeted = (
        [along_y(d) for d in range(1, n_gene)]
        + [along_in(d) for d in range(1, n_in)]
        + [along_out(d) for d in range(1, n_out)]
        + [after, before]
    )
    for target in greeted:
        pl.semaphore_signal(barrier, inc=1, device_id=target, device_id_type=MESH)

    mean = jnp.concatenate(
        [m.astype(F32) for m in split3(mean_ref[...][None, :])] + [jnp.zeros((5, mean_ref.shape[0]), F32)],
        axis=0,
    ).astype(BF16)
    brought[0].wait()
    turned = load_ref[...].T
    offset = jnp.sum(dot_nt(turned, mean), axis=1, keepdims=True)
    brought[1].wait()
    part_ref[:, rows:] = jnp.zeros((comps, wide - rows), F32)
    part_ref[:, :rows] = dot_nt(turned, expr_ref[...]) - offset
    pl.semaphore_wait(barrier, len(greeted))

    pending = []

    def send(src, dst, send_sem, recv_sem, target):
        copy = pltpu.make_async_remote_copy(
            src_ref=src,
            dst_ref=dst,
            send_sem=send_sem,
            recv_sem=recv_sem,
            device_id=target,
            device_id_type=MESH,
        )
        copy.start()
        pending.append(copy)
        return copy

    half = share // 2
    relay = n_gene == 8

    def share_of(d, start=0, size=share):
        at = lax.rem(gene + d, n_gene) * share + start
        return pl.ds(pl.multiple_of(at, half), size)

    own = share_of(0)
    routes = (
        (3, 0, share, 0, 1),
        (5, 0, share, 1, 7),
        (4, 0, half, 2, 2),
        (4, half, half, 2, 6),
        (1, 0, share, 3, 1),
        (7, 0, share, 4, 7),
    )
    if not relay:
        routes = tuple((d, 0, share, d - 1, d) for d in y_order)
    copies = [
        send(
            part_ref.at[share_of(d, start, size)],
            rs_slots.at[slot, pl.ds(start, size)],
            y_send.at[0, at],
            y_recv.at[0, at],
            along_y(to),
        )
        for at, (d, start, size, slot, to) in enumerate(routes)
    ]

    brought[2].wait()
    brought[3].wait()
    idx[...] = jnp.full(idx.shape, -(4 * rows), jnp.int32)
    idx[:NBR, :rows] = index_ref[...] - cell * rows
    live = lax.broadcasted_iota(jnp.int32, (NBR, rows), 0) < count_ref[...][None, :]
    kept = jnp.where(live, weight_ref[...], 0.0)
    wgt[...] = jnp.zeros_like(wgt)
    wgt[:NBR, :rows] = kept
    build_weights(rows, 1, idx, wgt, w_hi, w_lo)
    if relay:
        for copy in copies[:4]:
            copy.wait_recv()
        turn[0] = part_ref[share_of(2), :] + rs_slots[0]
        turn[0, :half] += rs_slots[2, :half]
        turn[1] = part_ref[share_of(6), :] + rs_slots[1]
        turn[1, half:] += rs_slots[2, half:]
        copies = copies[4:] + [
            send(turn.at[at], rs_slots.at[5 + at], y_send.at[0, 6 + at], y_recv.at[0, 6 + at], to)
            for at, to in enumerate((along_y(2), along_y(6)))
        ]
    build_weights(rows, 0, idx, wgt, w_hi, w_lo)
    inverse = 1.0 / (1.0 + jnp.sum(wgt[...], axis=0, keepdims=True))
    brought[4].wait()
    cents = centroid_ref[...]
    cent_norm = jnp.sqrt(jnp.sum(cents * cents, axis=1, keepdims=True) + EPSILON)
    cent_ref[...] = jnp.concatenate(
        [cents / cent_norm, jnp.zeros((n_gene * chunk - k_real, comps), F32)], axis=0
    ).astype(BF16)
    onehot = jnp.concatenate(
        [
            (batch_ref[...][None, :] == lax.broadcasted_iota(jnp.int32, (B, rows), 0)).astype(F32),
            jnp.zeros((B, wide - rows), F32),
        ],
        axis=1,
    )
    counts = jnp.sum(onehot, axis=1, keepdims=True)
    hot = onehot.astype(BF16)

    value = part_ref[own, :]
    for at, copy in enumerate(copies):
        copy.wait_recv()
        value += rs_slots[3 + at if relay else y_order[at] - 1]

    def spread(field, block):
        hi, lo = split2(field)
        span = slice(block * wide, (block + 1) * wide)
        both = dot(jnp.concatenate([hi, lo], axis=0), w_hi[span, :])
        return both[:share] + both[share:] + dot(hi, w_lo[span, :])

    for step in range(DIFF_STEPS):
        state[step] = value
        up = send(
            state.at[step], halo.at[step, 0], h_send.at[step, 0], h_recv.at[step, 0], after
        )
        down = send(
            state.at[step], halo.at[step, 1], h_send.at[step, 1], h_recv.at[step, 1], before
        )
        total = value + spread(value, 1)
        if step == 0:
            build_weights(rows, 2, idx, wgt, w_hi, w_lo)
        up.wait_recv()
        total += spread(halo[step, 0], 0)
        down.wait_recv()
        total += spread(halo[step, 1], 2)
        value = total * inverse

    full[own, :] = value

    def share_to(target, at, rows_at):
        return send(full.at[rows_at], full.at[rows_at], y_send.at[1, at], y_recv.at[1, at], target)

    smooth_v[...] = value[:, :rows]
    if relay:
        near = [share_to(along_y(d), at, own) for at, d in enumerate((2, 6, 1, 7))]
        near[0].wait_recv()
        near.append(share_to(along_y(2), 4, share_of(6, half, half)))
        near.append(share_to(along_y(1), 5, share_of(6)))
        near[1].wait_recv()
        near.append(share_to(along_y(6), 6, share_of(2, 0, half)))
        near.append(share_to(along_y(7), 7, share_of(2)))
        copies = near[2:]
    else:
        copies = [share_to(along_y(d), d - 1, own) for d in y_order]
    smooth_copy = pltpu.make_async_copy(smooth_v, smooth_ref, o_sem.at[0])
    smooth_copy.start()
    for copy in copies:
        copy.wait_recv()

    whole = full[...]
    norm = jnp.sqrt(jnp.sum(whole * whole, axis=0, keepdims=True) + EPSILON)
    unit[...] = (whole * (1.0 / norm)).astype(BF16)

    def kernel_rows(start):
        scores = dot(cent_ref[pl.ds(start, chunk), :], unit[...])
        number = lax.broadcasted_iota(jnp.int32, (chunk, wide), 0) + start
        return jnp.where(number < k_real, jnp.exp((scores - 1.0) * (2.0 / SIGMA_SCALE)), 0.0)

    def first(at, sums):
        start = pl.multiple_of(at * chunk, chunk)
        values = kernel_rows(start)
        hi, lo = split2(values)
        k_hi[pl.ds(start, chunk), :] = hi
        k_lo[pl.ds(start, chunk), :] = lo
        return sums + jnp.sum(values, axis=0, keepdims=True)

    sums = lax.fori_loop(0, n_gene, first, jnp.zeros((1, wide), F32))
    mine = pl.multiple_of(gene * chunk, chunk)
    kept_hi, kept_lo = k_hi[pl.ds(mine, chunk), :], k_lo[pl.ds(mine, chunk), :]
    hi, lo = split2(onehot / sums)
    observed = dot_nt(hi, kept_hi) + dot_nt(lo, kept_hi) + dot_nt(hi, kept_lo)
    column = lax.broadcasted_iota(jnp.int32, (B, chunk), 1) + gene * chunk
    fo_own[...] = jnp.where(column == n_gene * chunk - 1, counts, observed)

    def all_sum(source, slots, target_of, count, sems, at):
        send_sem, recv_sem = sems
        copies = []
        for d in farthest_first(count):
            copies.append(
                send(
                    source,
                    slots.at[d - 1],
                    send_sem.at[at, d - 1],
                    recv_sem.at[at, d - 1],
                    target_of(d),
                )
            )

        def finish():
            total = source[...]
            for d, copy in zip(farthest_first(count), copies):
                copy.wait_recv()
                total += slots[d - 1]
            return total

        return finish

    a_sems = (a_send, a_recv)
    fo_mid[...] = all_sum(fo_own, fo_in, along_in, n_in, a_sems, 0)()
    fo_all[gene] = all_sum(fo_mid, fo_out, along_out, n_out, a_sems, 1)()
    copies = []
    for d in y_order:
        copies.append(
            send(
                fo_all.at[gene],
                fo_all.at[gene],
                y_send.at[2, d - 1],
                y_recv.at[2, d - 1],
                along_y(d),
            )
        )
    for copy in copies:
        copy.wait_recv()

    sizes = fo_all[n_gene - 1][:, chunk - 1 : chunk]
    portion = sizes / jnp.sum(sizes, axis=0, keepdims=True)

    def penalty_of(seen):
        ratio = (jnp.sum(seen, axis=0, keepdims=True) * portion + 1.0) / (seen + 1.0)
        return jnp.concatenate(split3(ratio * ratio), axis=0)

    for at in range(n_gene):
        pen3[:, at * chunk : (at + 1) * chunk] = penalty_of(fo_all[at])
    parts = dot(pen3[...], k_hi[...]) + dot(pen3[...], k_lo[...])
    parts = (parts[:B] + parts[B : 2 * B]) + parts[2 * B :]
    weighted = jnp.sum(parts * onehot, axis=0, keepdims=True)
    lane = lax.broadcasted_iota(jnp.int32, (1, wide), 1)
    weighted = jnp.where(lane < rows, weighted, 1.0)
    factor = dot_tn(penalty_of(fo_all[gene]), jnp.concatenate([hot, hot, hot], axis=0))
    kernel_own = kept_hi.astype(F32) + kept_lo.astype(F32)
    response = (kernel_own * factor * (1.0 / weighted)).astype(BF16)
    cs[...] = dot_nt(response, unit[...])
    fb_own[...] = dot_nt(hot, response)

    c_copies = []
    for d in in_order:
        to = lax.rem(inner + d, n_in)
        c_copies.append(
            send(
                cs.at[pl.ds(pl.multiple_of(to * piece, piece), piece)],
                cs_in.at[d - 1],
                c_send.at[0, d - 1],
                c_recv.at[0, d - 1],
                along_in(d),
            )
        )
    fb_first = all_sum(fb_own, fb_in, along_in, n_in, a_sems, 2)
    piece_sum = cs[pl.ds(pl.multiple_of(inner * piece, piece), piece), :]
    for d, copy in zip(in_order, c_copies):
        copy.wait_recv()
        piece_sum += cs_in[d - 1]
    cs_mid[...] = piece_sum
    cs_second = all_sum(cs_mid, cs_out, along_out, n_out, (c_send, c_recv), 1)
    fb_mid[...] = fb_first()
    fb_second = all_sum(fb_mid, fb_out, along_out, n_out, a_sems, 3)
    piece_sum = cs_second()
    length = jnp.sqrt(jnp.sum(piece_sum * piece_sum, axis=1, keepdims=True) + EPSILON)

    new_cent_ref[gene, inner] = piece_sum / length
    copies = []
    for d in y_order:
        copies.append(
            send(
                new_cent_ref.at[gene, inner],
                new_cent_ref.at[gene, inner],
                y_send.at[4, d - 1],
                y_recv.at[4, d - 1],
                along_y(d),
            )
        )

    def piece_to(d, e, target):
        rows_at = (lax.rem(gene + n_gene - d, n_gene), inner)
        return send(
            new_cent_ref.at[rows_at],
            new_cent_ref.at[rows_at],
            x_send.at[e, d],
            x_recv.at[e, d],
            target,
        )

    x_order = farthest_first(n_x)
    x_copies = [[piece_to(0, e, along_in(2 * e))] for e in x_order]
    obs_ref[gene] = fb_second()
    obs_copies = []
    for d in y_order:
        obs_copies.append(
            send(
                obs_ref.at[gene],
                obs_ref.at[gene],
                y_send.at[3, d - 1],
                y_recv.at[3, d - 1],
                along_y(d),
            )
        )
    for d, copy in reversed(list(zip(y_order, copies))):
        copy.wait_recv()
        for e, group in zip(x_order, x_copies):
            group.append(piece_to(d, e, along_in(2 * e)))

    out_copies = [smooth_copy]

    def keep(number, at):
        copy = pltpu.make_async_copy(
            new_cent_ref.at[:, number], cent_out.at[:, number], o_sem.at[at]
        )
        copy.start()
        out_copies.append(copy)

    def to_twin(number, at):
        column = new_cent_ref.at[:, number]
        return send(column, column, t_send.at[at], t_recv.at[at], twin)

    shared = [to_twin(inner, 0)]
    keep(inner, 1)
    for e, group in zip(x_order, x_copies):
        for copy in group:
            copy.wait_recv()
        number = lax.rem(inner + n_in - 2 * e, n_in)
        shared.append(to_twin(number, e))
        keep(number, 1 + e)
    for copy in obs_copies:
        copy.wait_recv()
    for at in range(n_gene):
        size = min(chunk, k_real - at * chunk)
        obs_v[:, at * chunk : at * chunk + size] = obs_ref[at][:, :size]
    obs_copy = pltpu.make_async_copy(obs_v, obs_out, o_sem.at[1 + n_in])
    obs_copy.start()
    out_copies.append(obs_copy)
    other = inner + 1 - 2 * core
    for e, copy in zip([0] + x_order, shared):
        copy.wait_recv()
        keep(lax.rem(other + n_in - 2 * e, n_in), 1 + n_x + e)
    for copy in out_copies:
        copy.wait()
    for copy in pending:
        copy.wait_send()


def results_kernel(
    smooth_ref, cent_ref, obs_ref, smooth_out, cent_out, obs_out, smooth_v, cent_v, obs_v, sem
):
    k_real = cent_out.shape[0]
    parts = 4
    step = padded(-(-k_real // parts), 8)
    spans = [pl.ds(at * step, min(step, k_real - at * step)) for at in range(parts)]
    routes = [(cent_ref.at[span], cent_v.at[span], cent_out.at[span]) for span in spans]
    routes += [(smooth_ref, smooth_v, smooth_out), (obs_ref, obs_v, obs_out)]
    arriving = [
        pltpu.make_async_copy(a, b, sem.at[0, at]) for at, (a, b, _) in enumerate(routes)
    ]
    leaving = [
        pltpu.make_async_copy(b, c, sem.at[1, at]) for at, (_, b, c) in enumerate(routes)
    ]
    for copy in arriving:
        copy.start()
    for before, after in zip(arriving, leaving):
        before.wait()
        after.start()
    for copy in leaving:
        copy.wait()


def shards(n_in, expression, gene_mean, loadings, nbr_index, nbr_count, nbr_weight, batch, centroids):
    rows = expression.shape[0]
    comps = loadings.shape[1]
    k_real = centroids.shape[0]
    n_gene = lax.axis_size("gene")
    n_out = lax.axis_size("cell") // n_in
    wide = padded(rows)
    k_wide = padded(k_real)
    share = comps // n_gene
    chunk = k_wide // n_gene
    piece = chunk // n_in
    vmem = pl.BlockSpec(memory_space=pltpu.VMEM)
    hbm = pl.BlockSpec(memory_space=pltpu.HBM)
    dims = (rows, k_real, n_gene, n_in, n_out)
    dma = pltpu.SemaphoreType.DMA
    smooth, new_cent, obs = pl.pallas_call(
        functools.partial(main_kernel, dims),
        out_shape=[
            jax.ShapeDtypeStruct((share, rows), F32),
            jax.ShapeDtypeStruct((n_gene, n_in, piece, comps), F32),
            jax.ShapeDtypeStruct((B, k_real), F32),
        ],
        in_specs=[hbm, vmem, hbm, hbm, vmem, hbm, vmem, hbm],
        out_specs=[hbm] * 3,
        scratch_shapes=[
            pltpu.VMEM((n_gene, n_in, piece, comps), F32),
            pltpu.VMEM((n_gene, B, chunk), F32),
            pltpu.VMEM(expression.shape, BF16),
            pltpu.VMEM(loadings.shape, BF16),
            pltpu.VMEM((NBR, rows), jnp.int32),
            pltpu.VMEM((NBR, rows), F32),
            pltpu.VMEM(centroids.shape, F32),
            dma((5,)),
            pltpu.VMEM((comps, wide), F32),
            pltpu.VMEM((32, wide), jnp.int32),
            pltpu.VMEM((32, wide), F32),
            pltpu.VMEM((3 * wide, wide), BF16),
            pltpu.VMEM((3 * wide, wide), BF16),
            pltpu.VMEM((k_wide, comps), BF16),
            pltpu.VMEM((n_gene - 1, share, wide), F32),
            pltpu.VMEM((DIFF_STEPS, share, wide), F32),
            pltpu.VMEM((DIFF_STEPS, 2, share, wide), F32),
            pltpu.VMEM((comps, wide), F32),
            pltpu.VMEM((comps, wide), BF16),
            pltpu.VMEM((k_wide, wide), BF16),
            pltpu.VMEM((k_wide, wide), BF16),
            pltpu.VMEM((B, chunk), F32),
            pltpu.VMEM((max(n_in - 1, 1), B, chunk), F32),
            pltpu.VMEM((B, chunk), F32),
            pltpu.VMEM((max(n_out - 1, 1), B, chunk), F32),
            pltpu.VMEM((n_gene, B, chunk), F32),
            pltpu.VMEM((3 * B, k_wide), BF16),
            pltpu.VMEM((chunk, comps), F32),
            pltpu.VMEM((max(n_in - 1, 1), piece, comps), F32),
            pltpu.VMEM((piece, comps), F32),
            pltpu.VMEM((max(n_out - 1, 1), piece, comps), F32),
            pltpu.VMEM((B, chunk), F32),
            pltpu.VMEM((max(n_in - 1, 1), B, chunk), F32),
            pltpu.VMEM((B, chunk), F32),
            pltpu.VMEM((max(n_out - 1, 1), B, chunk), F32),
            dma((6, n_gene)),
            dma((6, n_gene)),
            dma((DIFF_STEPS, 2)),
            dma((DIFF_STEPS, 2)),
            dma((4, max(n_in, n_out) - 1)),
            dma((4, max(n_in, n_out) - 1)),
            dma((3, max(n_in, n_out) - 1)),
            dma((3, max(n_in, n_out) - 1)),
            dma((n_in // 2,)),
            dma((n_in // 2,)),
            dma((n_in // 2, n_gene)),
            dma((n_in // 2, n_gene)),
            dma((n_in + 2,)),
            pltpu.VMEM((2, share, wide), F32),
            pltpu.VMEM((share, rows), F32),
            pltpu.VMEM((B, k_real), F32),
        ],
        compiler_params=pltpu.CompilerParams(
            collective_id=0, has_side_effects=True, vmem_limit_bytes=60 * 1024 * 1024
        ),
    )(
        expression,
        gene_mean,
        loadings,
        nbr_index.T,
        nbr_count,
        nbr_weight.T,
        batch,
        centroids,
    )

    smooth, new_cent, obs = pl.pallas_call(
        results_kernel,
        out_shape=[
            jax.ShapeDtypeStruct((share, rows), F32),
            jax.ShapeDtypeStruct((k_real, comps), F32),
            jax.ShapeDtypeStruct((B, k_real), F32),
        ],
        in_specs=[hbm] * 3,
        out_specs=[hbm] * 3,
        scratch_shapes=[
            pltpu.VMEM((share, rows), F32),
            pltpu.VMEM((k_real, comps), F32),
            pltpu.VMEM((B, k_real), F32),
            dma((2, 6)),
        ],
        compiler_params=pltpu.CompilerParams(vmem_limit_bytes=60 * 1024 * 1024),
    )(smooth, new_cent.reshape(k_wide, comps), obs)
    return (smooth.T, new_cent, obs.T)


def solution(mesh):
    in_specs = (
        P("cell", "gene"),
        P("gene"),
        P("gene", None),
        P("cell", None),
        P("cell"),
        P("cell", None),
        P("cell"),
        P(),
    )
    out_specs = (P("cell", "gene"), P(), P())
    n_in = min(8, mesh.shape["cell"])
    body = functools.partial(shards, n_in)
    return jax.shard_map(body, mesh=mesh, in_specs=in_specs, out_specs=out_specs, check_vma=False)
```

```python
import functools

import jax
import jax.numpy as jnp
from jax import lax
from jax.experimental import pallas as pl
from jax.experimental.pallas import tpu as pltpu
from jax.sharding import PartitionSpec as P

B = 16
NBR = 30
DIFF_STEPS = 3
EPSILON = 1e-06
SIGMA_SCALE = 0.1
LANE = 128
MESH = pl.DeviceIdType.MESH
BF16 = jnp.bfloat16
F32 = jnp.float32


def padded(size, unit=LANE):
    return -(-size // unit) * unit


def split2(x):
    hi = x.astype(BF16)
    return hi, (x - hi.astype(F32)).astype(BF16)


def split3(x):
    hi = x.astype(BF16)
    rest = x - hi.astype(F32)
    mid = rest.astype(BF16)
    return hi, mid, (rest - mid.astype(F32)).astype(BF16)


def dot(a, b):
    return jnp.dot(a, b, preferred_element_type=F32)


def dot_nt(a, b):
    return lax.dot_general(a, b, (((1,), (1,)), ((), ())), preferred_element_type=F32)


def dot_tn(a, b):
    return lax.dot_general(a, b, (((0,), (0,)), ((), ())), preferred_element_type=F32)


def farthest_first(count):
    return sorted(range(1, count), key=lambda d: -min(d, count - d))


def build_weights(rows, block, index_ref, weight_ref, hi_ref, lo_ref, places=None):
    wide = hi_ref.shape[1]
    tile = LANE
    tiles = wide // tile
    base = block * wide
    for at in places or range(tiles):
        lanes = slice(at * tile, (at + 1) * tile)
        first, last = ((at, tiles), (0, tiles), (0, at + 1))[block]
        for low, high in ((0, first * tile), (min(last * tile, rows), wide)):
            if low < high:
                empty = jnp.zeros((high - low, tile), BF16)
                hi_ref[base + low : base + high, lanes] = empty
                lo_ref[base + low : base + high, lanes] = empty

        def rows_of(start, height, lanes=lanes):
            source = lax.broadcasted_iota(jnp.int32, (height, tile), 0) + (
                start + (block - 1) * rows
            )
            total = jnp.zeros((height, tile), F32)
            for slot in range(NBR):
                hit = index_ref[slot : slot + 1, lanes] == source
                total = jnp.where(hit, weight_ref[slot : slot + 1, lanes], total)
            hi, lo = split2(total)
            hi_ref[pl.ds(base + start, height), lanes] = hi
            lo_ref[pl.ds(base + start, height), lanes] = lo

        def fill(step, carry, rows_of=rows_of):
            rows_of(pl.multiple_of(step * tile, tile), tile)
            return carry

        lax.fori_loop(first, min(last, rows // tile), fill, 0)
        if last == tiles and rows % tile:
            rows_of(rows // tile * tile, rows % tile)


def main_kernel(
    dims,
    expr_hbm,
    mean_ref,
    load_hbm,
    index_hbm,
    count_ref,
    weight_hbm,
    batch_ref,
    centroid_hbm,
    smooth_ref,
    new_cent_ref,
    obs_out,
    obs_ref,
    expr_ref,
    load_ref,
    index_ref,
    weight_ref,
    centroid_ref,
    l_sem,
    part_ref,
    idx,
    wgt,
    w_hi,
    w_lo,
    cent_ref,
    rs_slots,
    state,
    halo,
    full,
    unit,
    k_hi,
    k_lo,
    fo_own,
    fo_in,
    fo_mid,
    fo_out,
    fo_all,
    pen3,
    cs,
    cs_in,
    cs_mid,
    cs_out,
    fb_own,
    fb_in,
    fb_mid,
    fb_out,
    y_send,
    y_recv,
    h_send,
    h_recv,
    a_send,
    a_recv,
    c_send,
    c_recv,
    t_send,
    t_recv,
    x_send,
    x_recv,
    turn,
):
    rows, k_real, n_gene, n_in, n_out = dims
    n_cell = n_in * n_out
    comps, wide = part_ref.shape
    y_order, in_order = farthest_first(n_gene), farthest_first(n_in)
    share = comps // n_gene
    chunk = cent_ref.shape[0] // n_gene
    piece = chunk // n_in
    n_x = n_in // 2
    cell = lax.axis_index("cell")
    gene = lax.axis_index("gene")
    inner = lax.rem(cell, n_in)
    outer = lax.div(cell, n_in)
    core = lax.rem(cell, 2)

    def along_y(d):
        return (cell, lax.rem(gene + d, n_gene))

    def along_in(d):
        return (outer * n_in + lax.rem(inner + d, n_in), gene)

    def along_out(d):
        return (lax.rem(outer + d, n_out) * n_in + inner, gene)

    after = (lax.rem(cell + 1, n_cell), gene)
    before = (lax.rem(cell + n_cell - 1, n_cell), gene)
    twin = (cell + 1 - 2 * core, gene)

    brought = [
        pltpu.make_async_copy(source, target, l_sem.at[at])
        for at, (source, target) in enumerate(
            (
                (load_hbm, load_ref),
                (expr_hbm, expr_ref),
                (index_hbm, index_ref),
                (weight_hbm, weight_ref),
                (centroid_hbm, centroid_ref),
            )
        )
    ]
    for copy in brought:
        copy.start()

    barrier = pltpu.get_barrier_semaphore()
    greeted = (
        [along_y(d) for d in range(1, n_gene)]
        + [along_in(d) for d in range(1, n_in)]
        + [along_out(d) for d in range(1, n_out)]
        + [after, before]
    )
    for target in greeted:
        pl.semaphore_signal(barrier, inc=1, device_id=target, device_id_type=MESH)

    mean = jnp.concatenate(
        [m.astype(F32) for m in split3(mean_ref[...][None, :])] + [jnp.zeros((5, mean_ref.shape[0]), F32)],
        axis=0,
    ).astype(BF16)
    brought[0].wait()
    turned = load_ref[...].T
    offset = jnp.sum(dot_nt(turned, mean), axis=1, keepdims=True)
    brought[1].wait()
    part_ref[:, rows:] = jnp.zeros((comps, wide - rows), F32)
    part_ref[:, :rows] = dot_nt(turned, expr_ref[...]) - offset
    pl.semaphore_wait(barrier, len(greeted))

    pending = []

    def send(src, dst, send_sem, recv_sem, target):
        copy = pltpu.make_async_remote_copy(
            src_ref=src,
            dst_ref=dst,
            send_sem=send_sem,
            recv_sem=recv_sem,
            device_id=target,
            device_id_type=MESH,
        )
        copy.start()
        pending.append(copy)
        return copy

    half = share // 2
    relay = n_gene == 8

    def share_of(d, start=0, size=share):
        at = lax.rem(gene + d, n_gene) * share + start
        return pl.ds(pl.multiple_of(at, half), size)

    own = share_of(0)
    routes = (
        (3, 0, share, 0, 1),
        (5, 0, share, 1, 7),
        (4, 0, half, 2, 2),
        (4, half, half, 2, 6),
        (1, 0, share, 3, 1),
        (7, 0, share, 4, 7),
    )
    if not relay:
        routes = tuple((d, 0, share, d - 1, d) for d in y_order)
    early = 4 if relay else len(routes)

    def send_route(at):
        d, start, size, slot, to = routes[at]
        return send(
            part_ref.at[share_of(d, start, size)],
            rs_slots.at[slot, pl.ds(start, size)],
            y_send.at[0, at],
            y_recv.at[0, at],
            along_y(to),
        )

    copies = [send_route(at) for at in range(early)]

    brought[2].wait()
    brought[3].wait()
    idx[...] = jnp.full(idx.shape, -(4 * rows), jnp.int32)
    idx[:NBR, :rows] = index_ref[...] - cell * rows
    live = lax.broadcasted_iota(jnp.int32, (NBR, rows), 0) < count_ref[...][None, :]
    kept = jnp.where(live, weight_ref[...], 0.0)
    wgt[...] = jnp.zeros_like(wgt)
    wgt[:NBR, :rows] = kept
    inverse = 1.0 / (1.0 + jnp.sum(wgt[...], axis=0, keepdims=True))
    merged = jnp.zeros(wgt.shape, F32)
    for slot in range(NBR):
        same = idx[...] == idx[slot : slot + 1, :]
        merged += jnp.where(same, wgt[slot : slot + 1, :], 0.0)
    wgt[...] = merged
    build_weights(rows, 1, idx, wgt, w_hi, w_lo, range(2))
    copies += [send_route(at) for at in range(early, len(routes))]
    build_weights(rows, 1, idx, wgt, w_hi, w_lo, range(2, wide // LANE))
    if relay:
        for copy in copies[:4]:
            copy.wait_recv()
        turn[0] = part_ref[share_of(2), :] + rs_slots[0]
        turn[0, :half] += rs_slots[2, :half]
        turn[1] = part_ref[share_of(6), :] + rs_slots[1]
        turn[1, half:] += rs_slots[2, half:]
        copies = copies[4:] + [
            send(turn.at[at], rs_slots.at[5 + at], y_send.at[0, 6 + at], y_recv.at[0, 6 + at], to)
            for at, to in enumerate((along_y(2), along_y(6)))
        ]
    build_weights(rows, 0, idx, wgt, w_hi, w_lo)
    brought[4].wait()
    cents = centroid_ref[...]
    cent_norm = jnp.sqrt(jnp.sum(cents * cents, axis=1, keepdims=True) + EPSILON)
    cent_ref[...] = jnp.concatenate(
        [cents / cent_norm, jnp.zeros((n_gene * chunk - k_real, comps), F32)], axis=0
    ).astype(BF16)
    onehot = jnp.concatenate(
        [
            (batch_ref[...][None, :] == lax.broadcasted_iota(jnp.int32, (B, rows), 0)).astype(F32),
            jnp.zeros((B, wide - rows), F32),
        ],
        axis=1,
    )
    counts = jnp.sum(onehot, axis=1, keepdims=True)
    hot = onehot.astype(BF16)

    value = part_ref[own, :]
    for at, copy in enumerate(copies):
        copy.wait_recv()
        value += rs_slots[3 + at if relay else y_order[at] - 1]

    def spread(field, block):
        hi, lo = split2(field)
        pair = jnp.concatenate([hi, lo], axis=0)
        base = block * wide
        found = []
        for low in range(0, wide, 2 * LANE):
            high = min(low + 2 * LANE, wide)
            first, last = ((low, wide), (0, wide), (0, high))[block]
            span, lanes = slice(base + first, base + last), slice(low, high)
            both = dot(pair[:, first:last], w_hi[span, lanes])
            found.append(both[:share] + both[share:] + dot(hi[:, first:last], w_lo[span, lanes]))
        return jnp.concatenate(found, axis=1)

    for step in range(DIFF_STEPS):
        state[step] = value
        up = send(
            state.at[step], halo.at[step, 0], h_send.at[step, 0], h_recv.at[step, 0], after
        )
        down = send(
            state.at[step], halo.at[step, 1], h_send.at[step, 1], h_recv.at[step, 1], before
        )
        total = value + spread(value, 1)
        if step == 0:
            build_weights(rows, 2, idx, wgt, w_hi, w_lo)
        up.wait_recv()
        total += spread(halo[step, 0], 0)
        down.wait_recv()
        total += spread(halo[step, 1], 2)
        value = total * inverse

    full[own, :] = value

    cut = padded(wide * 3 // 5)
    spans = ((0, cut), (cut, wide - cut))

    def share_to(target, at, rows_at, part):
        place = full.at[rows_at, pl.ds(*spans[part])]
        return send(place, place, y_send.at[1 + 4 * part, at], y_recv.at[1 + 4 * part, at], target)

    smooth_ref[...] = value[:, :rows]
    if relay:
        near = [
            [share_to(along_y(d), at, own, part) for at, d in enumerate((2, 6, 1, 7))]
            for part in range(2)
        ]
        arrivals = []
        for part in range(2):
            one, two = near[part][:2]
            one.wait_recv()
            far = [
                share_to(along_y(2), 4, share_of(6, half, half), part),
                share_to(along_y(1), 5, share_of(6), part),
            ]
            two.wait_recv()
            far.append(share_to(along_y(6), 6, share_of(2, 0, half), part))
            far.append(share_to(along_y(7), 7, share_of(2), part))
            arrivals.append(near[part][2:] + far)
    else:
        arrivals = [[share_to(along_y(d), d - 1, own, part) for d in y_order] for part in range(2)]

    found = []
    for part in range(2):
        low, size = spans[part]
        lanes = slice(low, low + size)
        for copy in arrivals[part]:
            copy.wait_recv()
        whole = full[:, lanes]
        norm = jnp.sqrt(jnp.sum(whole * whole, axis=0, keepdims=True) + EPSILON)
        unit[:, lanes] = (whole * (1.0 / norm)).astype(BF16)

        def first(at, sums, lanes=lanes, size=size):
            start = pl.multiple_of(at * chunk, chunk)
            scores = dot(cent_ref[pl.ds(start, chunk), :], unit[:, lanes])
            number = lax.broadcasted_iota(jnp.int32, (chunk, size), 0) + start
            values = jnp.exp((scores - 1.0) * (2.0 / SIGMA_SCALE))
            values = jnp.where(number < k_real, values, 0.0)
            hi, lo = split2(values)
            k_hi[pl.ds(start, chunk), lanes] = hi
            k_lo[pl.ds(start, chunk), lanes] = lo
            return sums + jnp.sum(values, axis=0, keepdims=True)

        found.append(lax.fori_loop(0, n_gene, first, jnp.zeros((1, size), F32)))
    sums = jnp.concatenate(found, axis=1)
    mine = pl.multiple_of(gene * chunk, chunk)
    kept_hi, kept_lo = k_hi[pl.ds(mine, chunk), :], k_lo[pl.ds(mine, chunk), :]
    hi, lo = split2(onehot / sums)
    observed = dot_nt(hi, kept_hi) + dot_nt(lo, kept_hi) + dot_nt(hi, kept_lo)
    column = lax.broadcasted_iota(jnp.int32, (B, chunk), 1) + gene * chunk
    fo_own[...] = jnp.where(column == n_gene * chunk - 1, counts, observed)

    def all_sum(source, slots, target_of, count, sems, at):
        send_sem, recv_sem = sems
        copies = []
        for d in farthest_first(count):
            copies.append(
                send(
                    source,
                    slots.at[d - 1],
                    send_sem.at[at, d - 1],
                    recv_sem.at[at, d - 1],
                    target_of(d),
                )
            )

        def finish():
            total = source[...]
            for d, copy in zip(farthest_first(count), copies):
                copy.wait_recv()
                total += slots[d - 1]
            return total

        return finish

    a_sems = (a_send, a_recv)
    fo_mid[...] = all_sum(fo_own, fo_in, along_in, n_in, a_sems, 0)()
    fo_all[gene] = all_sum(fo_mid, fo_out, along_out, n_out, a_sems, 1)()
    copies = []
    for d in y_order:
        copies.append(
            send(
                fo_all.at[gene],
                fo_all.at[gene],
                y_send.at[2, d - 1],
                y_recv.at[2, d - 1],
                along_y(d),
            )
        )
    for copy in copies:
        copy.wait_recv()

    sizes = fo_all[n_gene - 1][:, chunk - 1 : chunk]
    portion = sizes / jnp.sum(sizes, axis=0, keepdims=True)

    def penalty_of(seen):
        ratio = (jnp.sum(seen, axis=0, keepdims=True) * portion + 1.0) / (seen + 1.0)
        return jnp.concatenate(split3(ratio * ratio), axis=0)

    for at in range(n_gene):
        pen3[:, at * chunk : (at + 1) * chunk] = penalty_of(fo_all[at])
    parts = dot(pen3[...], k_hi[...]) + dot(pen3[...], k_lo[...])
    parts = (parts[:B] + parts[B : 2 * B]) + parts[2 * B :]
    weighted = jnp.sum(parts * onehot, axis=0, keepdims=True)
    lane = lax.broadcasted_iota(jnp.int32, (1, wide), 1)
    weighted = jnp.where(lane < rows, weighted, 1.0)
    factor = dot_tn(penalty_of(fo_all[gene]), jnp.concatenate([hot, hot, hot], axis=0))
    kernel_own = kept_hi.astype(F32) + kept_lo.astype(F32)
    response = (kernel_own * factor * (1.0 / weighted)).astype(BF16)
    cs[...] = dot_nt(response, unit[...])
    fb_own[...] = dot_nt(hot, response)

    c_copies = []
    for d in in_order:
        to = lax.rem(inner + d, n_in)
        c_copies.append(
            send(
                cs.at[pl.ds(pl.multiple_of(to * piece, piece), piece)],
                cs_in.at[d - 1],
                c_send.at[0, d - 1],
                c_recv.at[0, d - 1],
                along_in(d),
            )
        )
    piece_sum = cs[pl.ds(pl.multiple_of(inner * piece, piece), piece), :]
    for d, copy in zip(in_order, c_copies):
        copy.wait_recv()
        piece_sum += cs_in[d - 1]
    cs_mid[...] = piece_sum
    cs_second = all_sum(cs_mid, cs_out, along_out, n_out, (c_send, c_recv), 1)
    fb_first = all_sum(fb_own, fb_in, along_in, n_in, a_sems, 2)
    fb_mid[...] = fb_first()
    fb_second = all_sum(fb_mid, fb_out, along_out, n_out, a_sems, 3)
    piece_sum = cs_second()
    length = jnp.sqrt(jnp.sum(piece_sum * piece_sum, axis=1, keepdims=True) + EPSILON)

    new_cent_ref[gene, inner] = piece_sum / length
    copies = []
    for d in y_order:
        copies.append(
            send(
                new_cent_ref.at[gene, inner],
                new_cent_ref.at[gene, inner],
                y_send.at[4, d - 1],
                y_recv.at[4, d - 1],
                along_y(d),
            )
        )

    def piece_to(d, e, target):
        rows_at = (lax.rem(gene + n_gene - d, n_gene), inner)
        return send(
            new_cent_ref.at[rows_at],
            new_cent_ref.at[rows_at],
            x_send.at[e, d],
            x_recv.at[e, d],
            target,
        )

    x_order = farthest_first(n_x)
    x_copies = [[piece_to(0, e, along_in(2 * e))] for e in x_order]
    obs_ref[gene] = fb_second()
    obs_copies = []
    for d in y_order:
        obs_copies.append(
            send(
                obs_ref.at[gene],
                obs_ref.at[gene],
                y_send.at[3, d - 1],
                y_recv.at[3, d - 1],
                along_y(d),
            )
        )
    for d, copy in reversed(list(zip(y_order, copies))):
        copy.wait_recv()
        for e, group in zip(x_order, x_copies):
            group.append(piece_to(d, e, along_in(2 * e)))

    def to_twin(number, at):
        column = new_cent_ref.at[:, number]
        return send(column, column, t_send.at[at], t_recv.at[at], twin)

    shared = [to_twin(inner, 0)]
    for e, group in zip(x_order, x_copies):
        for copy in group:
            copy.wait_recv()
        number = lax.rem(inner + n_in - 2 * e, n_in)
        shared.append(to_twin(number, e))
    for copy in obs_copies:
        copy.wait_recv()
    for at in range(n_gene):
        size = min(chunk, k_real - at * chunk)
        obs_out[:, at * chunk : at * chunk + size] = obs_ref[at][:, :size]
    for copy in shared:
        copy.wait_recv()
    for copy in pending:
        copy.wait_send()


def results_kernel(smooth_ref, cent_ref, obs_ref, smooth_out, cent_out, obs_out, sem):
    routes = (
        (cent_ref.at[pl.ds(0, cent_out.shape[0])], cent_out),
        (smooth_ref, smooth_out),
        (obs_ref, obs_out),
    )
    copies = [pltpu.make_async_copy(a, b, sem.at[at]) for at, (a, b) in enumerate(routes)]
    for copy in copies:
        copy.start()
    for copy in copies:
        copy.wait()


def shards(n_in, expression, gene_mean, loadings, nbr_index, nbr_count, nbr_weight, batch, centroids):
    rows = expression.shape[0]
    comps = loadings.shape[1]
    k_real = centroids.shape[0]
    n_gene = lax.axis_size("gene")
    n_out = lax.axis_size("cell") // n_in
    wide = padded(rows)
    k_wide = padded(k_real)
    share = comps // n_gene
    chunk = k_wide // n_gene
    piece = chunk // n_in
    vmem = pl.BlockSpec(memory_space=pltpu.VMEM)
    hbm = pl.BlockSpec(memory_space=pltpu.HBM)
    dims = (rows, k_real, n_gene, n_in, n_out)
    dma = pltpu.SemaphoreType.DMA
    smooth, new_cent, obs = pl.pallas_call(
        functools.partial(main_kernel, dims),
        out_shape=[
            pltpu.VMEM((share, rows), F32),
            pltpu.VMEM((n_gene, n_in, piece, comps), F32),
            pltpu.VMEM((B, k_real), F32),
        ],
        in_specs=[hbm, vmem, hbm, hbm, vmem, hbm, vmem, hbm],
        out_specs=[vmem] * 3,
        scratch_shapes=[
            pltpu.VMEM((n_gene, B, chunk), F32),
            pltpu.VMEM(expression.shape, BF16),
            pltpu.VMEM(loadings.shape, BF16),
            pltpu.VMEM((NBR, rows), jnp.int32),
            pltpu.VMEM((NBR, rows), F32),
            pltpu.VMEM(centroids.shape, F32),
            dma((5,)),
            pltpu.VMEM((comps, wide), F32),
            pltpu.VMEM((32, wide), jnp.int32),
            pltpu.VMEM((32, wide), F32),
            pltpu.VMEM((3 * wide, wide), BF16),
            pltpu.VMEM((3 * wide, wide), BF16),
            pltpu.VMEM((k_wide, comps), BF16),
            pltpu.VMEM((n_gene - 1, share, wide), F32),
            pltpu.VMEM((DIFF_STEPS, share, wide), F32),
            pltpu.VMEM((DIFF_STEPS, 2, share, wide), F32),
            pltpu.VMEM((comps, wide), F32),
            pltpu.VMEM((comps, wide), BF16),
            pltpu.VMEM((k_wide, wide), BF16),
            pltpu.VMEM((k_wide, wide), BF16),
            pltpu.VMEM((B, chunk), F32),
            pltpu.VMEM((max(n_in - 1, 1), B, chunk), F32),
            pltpu.VMEM((B, chunk), F32),
            pltpu.VMEM((max(n_out - 1, 1), B, chunk), F32),
            pltpu.VMEM((n_gene, B, chunk), F32),
            pltpu.VMEM((3 * B, k_wide), BF16),
            pltpu.VMEM((chunk, comps), F32),
            pltpu.VMEM((max(n_in - 1, 1), piece, comps), F32),
            pltpu.VMEM((piece, comps), F32),
            pltpu.VMEM((max(n_out - 1, 1), piece, comps), F32),
            pltpu.VMEM((B, chunk), F32),
            pltpu.VMEM((max(n_in - 1, 1), B, chunk), F32),
            pltpu.VMEM((B, chunk), F32),
            pltpu.VMEM((max(n_out - 1, 1), B, chunk), F32),
            dma((6, n_gene)),
            dma((6, n_gene)),
            dma((DIFF_STEPS, 2)),
            dma((DIFF_STEPS, 2)),
            dma((4, max(n_in, n_out) - 1)),
            dma((4, max(n_in, n_out) - 1)),
            dma((3, max(n_in, n_out) - 1)),
            dma((3, max(n_in, n_out) - 1)),
            dma((n_in // 2,)),
            dma((n_in // 2,)),
            dma((n_in // 2, n_gene)),
            dma((n_in // 2, n_gene)),
            pltpu.VMEM((2, share, wide), F32),
        ],
        compiler_params=pltpu.CompilerParams(
            collective_id=0, has_side_effects=True, vmem_limit_bytes=60 * 1024 * 1024
        ),
    )(
        expression,
        gene_mean,
        loadings,
        nbr_index.T,
        nbr_count,
        nbr_weight.T,
        batch,
        centroids,
    )

    smooth, new_cent, obs = pl.pallas_call(
        results_kernel,
        out_shape=[
            jax.ShapeDtypeStruct((share, rows), F32),
            jax.ShapeDtypeStruct((k_real, comps), F32),
            jax.ShapeDtypeStruct((B, k_real), F32),
        ],
        in_specs=[vmem] * 3,
        out_specs=[hbm] * 3,
        scratch_shapes=[dma((3,))],
        compiler_params=pltpu.CompilerParams(vmem_limit_bytes=32 * 1024 * 1024),
    )(smooth, new_cent.reshape(k_wide, comps), obs)
    return (smooth.T, new_cent, obs.T)


def solution(mesh):
    in_specs = (
        P("cell", "gene"),
        P("gene"),
        P("gene", None),
        P("cell", None),
        P("cell"),
        P("cell", None),
        P("cell"),
        P(),
    )
    out_specs = (P("cell", "gene"), P(), P())
    n_in = min(8, mesh.shape["cell"])
    body = functools.partial(shards, n_in)
    return jax.shard_map(body, mesh=mesh, in_specs=in_specs, out_specs=out_specs, check_vma=False)
```

```python
import functools

import jax
import jax.numpy as jnp
from jax import lax
from jax.experimental import pallas as pl
from jax.experimental.pallas import tpu as pltpu
from jax.sharding import PartitionSpec as P

B = 16
NBR = 30
DIFF_STEPS = 3
EPSILON = 1e-06
SIGMA_SCALE = 0.1
LANE = 128
MESH = pl.DeviceIdType.MESH
BF16 = jnp.bfloat16
F32 = jnp.float32


def padded(size, unit=LANE):
    return -(-size // unit) * unit


def split2(x):
    hi = x.astype(BF16)
    return hi, (x - hi.astype(F32)).astype(BF16)


def split3(x):
    hi = x.astype(BF16)
    rest = x - hi.astype(F32)
    mid = rest.astype(BF16)
    return hi, mid, (rest - mid.astype(F32)).astype(BF16)


def dot(a, b):
    return jnp.dot(a, b, preferred_element_type=F32)


def dot_nt(a, b):
    return lax.dot_general(a, b, (((1,), (1,)), ((), ())), preferred_element_type=F32)


def dot_tn(a, b):
    return lax.dot_general(a, b, (((0,), (0,)), ((), ())), preferred_element_type=F32)


def farthest_first(count):
    return sorted(range(1, count), key=lambda d: -min(d, count - d))


def build_weights(rows, block, index_ref, weight_ref, hi_ref, lo_ref, places=None):
    wide = hi_ref.shape[1]
    tile = LANE
    tiles = wide // tile
    base = block * wide
    for at in places or range(tiles):
        lanes = slice(at * tile, (at + 1) * tile)
        first, last = ((at, tiles), (0, tiles), (0, at + 1))[block]
        for low, high in ((0, first * tile), (min(last * tile, rows), wide)):
            if low < high:
                empty = jnp.zeros((high - low, tile), BF16)
                hi_ref[base + low : base + high, lanes] = empty
                lo_ref[base + low : base + high, lanes] = empty

        def rows_of(start, height, lanes=lanes):
            source = lax.broadcasted_iota(jnp.int32, (height, tile), 0) + (
                start + (block - 1) * rows
            )
            total = jnp.zeros((height, tile), F32)
            for slot in range(NBR):
                hit = index_ref[slot : slot + 1, lanes] == source
                total = jnp.where(hit, weight_ref[slot : slot + 1, lanes], total)
            hi, lo = split2(total)
            hi_ref[pl.ds(base + start, height), lanes] = hi
            lo_ref[pl.ds(base + start, height), lanes] = lo

        def fill(step, carry, rows_of=rows_of):
            rows_of(pl.multiple_of(step * tile, tile), tile)
            return carry

        lax.fori_loop(first, min(last, rows // tile), fill, 0)
        if last == tiles and rows % tile:
            rows_of(rows // tile * tile, rows % tile)


def main_kernel(
    dims,
    expr_hbm,
    mean_ref,
    load_hbm,
    index_hbm,
    count_ref,
    weight_hbm,
    batch_ref,
    centroid_hbm,
    smooth_ref,
    new_cent_ref,
    obs_out,
    obs_ref,
    expr_ref,
    load_ref,
    index_ref,
    weight_ref,
    centroid_ref,
    l_sem,
    part_ref,
    idx,
    wgt,
    w_hi,
    w_lo,
    cent_ref,
    rs_slots,
    state,
    halo,
    full,
    unit,
    k_hi,
    k_lo,
    fo_own,
    fo_in,
    fo_mid,
    fo_out,
    fo_all,
    pen3,
    cs,
    cs_in,
    cs_mid,
    cs_out,
    fb_own,
    fb_in,
    fb_mid,
    fb_out,
    y_send,
    y_recv,
    h_send,
    h_recv,
    a_send,
    a_recv,
    c_send,
    c_recv,
    t_send,
    t_recv,
    x_send,
    x_recv,
    turn,
):
    rows, k_real, n_gene, n_in, n_out = dims
    n_cell = n_in * n_out
    comps, wide = part_ref.shape
    y_order, in_order = farthest_first(n_gene), farthest_first(n_in)
    share = comps // n_gene
    chunk = cent_ref.shape[0] // n_gene
    piece = chunk // n_in
    n_x = n_in // 2
    cell = lax.axis_index("cell")
    gene = lax.axis_index("gene")
    inner = lax.rem(cell, n_in)
    outer = lax.div(cell, n_in)
    core = lax.rem(cell, 2)

    def along_y(d):
        return (cell, lax.rem(gene + d, n_gene))

    def along_in(d):
        return (outer * n_in + lax.rem(inner + d, n_in), gene)

    def along_out(d):
        return (lax.rem(outer + d, n_out) * n_in + inner, gene)

    after = (lax.rem(cell + 1, n_cell), gene)
    before = (lax.rem(cell + n_cell - 1, n_cell), gene)
    twin = (cell + 1 - 2 * core, gene)

    brought = [
        pltpu.make_async_copy(source, target, l_sem.at[at])
        for at, (source, target) in enumerate(
            (
                (load_hbm, load_ref),
                (expr_hbm, expr_ref),
                (index_hbm, index_ref),
                (weight_hbm, weight_ref),
                (centroid_hbm, centroid_ref),
            )
        )
    ]
    for copy in brought:
        copy.start()

    barrier = pltpu.get_barrier_semaphore()
    greeted = (
        [along_y(d) for d in range(1, n_gene)]
        + [along_in(d) for d in range(1, n_in)]
        + [along_out(d) for d in range(1, n_out)]
        + [after, before]
    )
    for target in greeted:
        pl.semaphore_signal(barrier, inc=1, device_id=target, device_id_type=MESH)

    mean = jnp.concatenate(
        [m.astype(F32) for m in split3(mean_ref[...][None, :])] + [jnp.zeros((5, mean_ref.shape[0]), F32)],
        axis=0,
    ).astype(BF16)
    brought[0].wait()
    turned = load_ref[...].T
    offset = jnp.sum(dot_nt(turned, mean), axis=1, keepdims=True)
    brought[1].wait()
    part_ref[:, rows:] = jnp.zeros((comps, wide - rows), F32)
    part_ref[:, :rows] = dot_nt(turned, expr_ref[...]) - offset
    pl.semaphore_wait(barrier, len(greeted))

    pending = []

    def send(src, dst, send_sem, recv_sem, target):
        copy = pltpu.make_async_remote_copy(
            src_ref=src,
            dst_ref=dst,
            send_sem=send_sem,
            recv_sem=recv_sem,
            device_id=target,
            device_id_type=MESH,
        )
        copy.start()
        pending.append(copy)
        return copy

    def settle(latest):
        while len(pending) > latest:
            pending.pop(0).wait_send()

    half = share // 2
    relay = n_gene == 8

    def share_of(d, start=0, size=share):
        at = lax.rem(gene + d, n_gene) * share + start
        return pl.ds(pl.multiple_of(at, half), size)

    own = share_of(0)
    routes = (
        (3, 0, share, 0, 1),
        (5, 0, share, 1, 7),
        (4, 0, half, 2, 2),
        (4, half, half, 2, 6),
        (1, 0, share, 3, 1),
        (7, 0, share, 4, 7),
    )
    if not relay:
        routes = tuple((d, 0, share, d - 1, d) for d in y_order)
    early = 4 if relay else len(routes)

    def send_route(at):
        d, start, size, slot, to = routes[at]
        return send(
            part_ref.at[share_of(d, start, size)],
            rs_slots.at[slot, pl.ds(start, size)],
            y_send.at[0, at],
            y_recv.at[0, at],
            along_y(to),
        )

    copies = [send_route(at) for at in range(early)]

    brought[2].wait()
    brought[3].wait()
    idx[...] = jnp.full(idx.shape, -(4 * rows), jnp.int32)
    idx[:NBR, :rows] = index_ref[...] - cell * rows
    live = lax.broadcasted_iota(jnp.int32, (NBR, rows), 0) < count_ref[...][None, :]
    kept = jnp.where(live, weight_ref[...], 0.0)
    wgt[...] = jnp.zeros_like(wgt)
    wgt[:NBR, :rows] = kept
    inverse = 1.0 / (1.0 + jnp.sum(wgt[...], axis=0, keepdims=True))
    merged = jnp.zeros(wgt.shape, F32)
    for slot in range(NBR):
        same = idx[...] == idx[slot : slot + 1, :]
        merged += jnp.where(same, wgt[slot : slot + 1, :], 0.0)
    wgt[...] = merged
    build_weights(rows, 1, idx, wgt, w_hi, w_lo, range(2))
    copies += [send_route(at) for at in range(early, len(routes))]
    build_weights(rows, 1, idx, wgt, w_hi, w_lo, range(2, wide // LANE))
    if relay:
        for copy in copies[:4]:
            copy.wait_recv()
        turn[0] = part_ref[share_of(2), :] + rs_slots[0]
        turn[0, :half] += rs_slots[2, :half]
        turn[1] = part_ref[share_of(6), :] + rs_slots[1]
        turn[1, half:] += rs_slots[2, half:]
        copies = copies[4:] + [
            send(turn.at[at], rs_slots.at[5 + at], y_send.at[0, 6 + at], y_recv.at[0, 6 + at], to)
            for at, to in enumerate((along_y(2), along_y(6)))
        ]
    build_weights(rows, 0, idx, wgt, w_hi, w_lo)
    brought[4].wait()
    cents = centroid_ref[...]
    cent_norm = jnp.sqrt(jnp.sum(cents * cents, axis=1, keepdims=True) + EPSILON)
    cent_ref[...] = jnp.concatenate(
        [cents / cent_norm, jnp.zeros((n_gene * chunk - k_real, comps), F32)], axis=0
    ).astype(BF16)
    onehot = jnp.concatenate(
        [
            (batch_ref[...][None, :] == lax.broadcasted_iota(jnp.int32, (B, rows), 0)).astype(F32),
            jnp.zeros((B, wide - rows), F32),
        ],
        axis=1,
    )
    counts = jnp.sum(onehot, axis=1, keepdims=True)
    hot = onehot.astype(BF16)

    value = part_ref[own, :]
    for at, copy in enumerate(copies):
        copy.wait_recv()
        value += rs_slots[3 + at if relay else y_order[at] - 1]

    def spread(field, block):
        hi, lo = split2(field)
        pair = jnp.concatenate([hi, lo], axis=0)
        base = block * wide
        found = []
        for low in range(0, wide, 2 * LANE):
            high = min(low + 2 * LANE, wide)
            first, last = ((low, wide), (0, wide), (0, high))[block]
            span, lanes = slice(base + first, base + last), slice(low, high)
            both = dot(pair[:, first:last], w_hi[span, lanes])
            found.append(both[:share] + both[share:] + dot(hi[:, first:last], w_lo[span, lanes]))
        return jnp.concatenate(found, axis=1)

    for step in range(DIFF_STEPS):
        state[step] = value
        up = send(
            state.at[step], halo.at[step, 0], h_send.at[step, 0], h_recv.at[step, 0], after
        )
        down = send(
            state.at[step], halo.at[step, 1], h_send.at[step, 1], h_recv.at[step, 1], before
        )
        total = value + spread(value, 1)
        if step == 0:
            build_weights(rows, 2, idx, wgt, w_hi, w_lo)
        settle(2)
        up.wait_recv()
        total += spread(halo[step, 0], 0)
        down.wait_recv()
        total += spread(halo[step, 1], 2)
        value = total * inverse

    full[own, :] = value

    cut = padded(wide * 3 // 5)
    spans = ((0, cut), (cut, wide - cut))

    def share_to(target, at, rows_at, part):
        place = full.at[rows_at, pl.ds(*spans[part])]
        return send(place, place, y_send.at[1 + 4 * part, at], y_recv.at[1 + 4 * part, at], target)

    if relay:
        near = [
            [share_to(along_y(d), at, own, part) for at, d in enumerate((2, 6, 1, 7))]
            for part in range(2)
        ]
        arrivals = []
        for part in range(2):
            one, two = near[part][:2]
            one.wait_recv()
            far = [
                share_to(along_y(2), 4, share_of(6, half, half), part),
                share_to(along_y(1), 5, share_of(6), part),
            ]
            two.wait_recv()
            far.append(share_to(along_y(6), 6, share_of(2, 0, half), part))
            far.append(share_to(along_y(7), 7, share_of(2), part))
            arrivals.append(near[part][2:] + far)
    else:
        arrivals = [[share_to(along_y(d), d - 1, own, part) for d in y_order] for part in range(2)]

    smooth_ref[...] = value[:, :rows]

    settle(16 if relay else 2 * len(y_order))
    found = []
    for part in range(2):
        low, size = spans[part]
        lanes = slice(low, low + size)
        for copy in arrivals[part]:
            copy.wait_recv()
        whole = full[:, lanes]
        norm = jnp.sqrt(jnp.sum(whole * whole, axis=0, keepdims=True) + EPSILON)
        unit[:, lanes] = (whole * (1.0 / norm)).astype(BF16)

        def first(at, sums, lanes=lanes, size=size):
            start = pl.multiple_of(at * chunk, chunk)
            scores = dot(cent_ref[pl.ds(start, chunk), :], unit[:, lanes])
            number = lax.broadcasted_iota(jnp.int32, (chunk, size), 0) + start
            values = jnp.exp((scores - 1.0) * (2.0 / SIGMA_SCALE))
            values = jnp.where(number < k_real, values, 0.0)
            hi, lo = split2(values)
            k_hi[pl.ds(start, chunk), lanes] = hi
            k_lo[pl.ds(start, chunk), lanes] = lo
            return sums + jnp.sum(values, axis=0, keepdims=True)

        found.append(lax.fori_loop(0, n_gene, first, jnp.zeros((1, size), F32)))
    sums = jnp.concatenate(found, axis=1)
    mine = pl.multiple_of(gene * chunk, chunk)
    kept_hi, kept_lo = k_hi[pl.ds(mine, chunk), :], k_lo[pl.ds(mine, chunk), :]
    hi, lo = split2(onehot / sums)
    observed = dot_nt(hi, kept_hi) + dot_nt(lo, kept_hi) + dot_nt(hi, kept_lo)
    column = lax.broadcasted_iota(jnp.int32, (B, chunk), 1) + gene * chunk
    fo_own[...] = jnp.where(column == n_gene * chunk - 1, counts, observed)

    def all_sum(source, slots, target_of, count, sems, at):
        send_sem, recv_sem = sems
        copies = []
        for d in farthest_first(count):
            copies.append(
                send(
                    source,
                    slots.at[d - 1],
                    send_sem.at[at, d - 1],
                    recv_sem.at[at, d - 1],
                    target_of(d),
                )
            )

        def finish(latest=count - 1):
            settle(latest)
            total = source[...]
            for d, copy in zip(farthest_first(count), copies):
                copy.wait_recv()
                total += slots[d - 1]
            return total

        return finish

    a_sems = (a_send, a_recv)
    fo_mid[...] = all_sum(fo_own, fo_in, along_in, n_in, a_sems, 0)()
    fo_all[gene] = all_sum(fo_mid, fo_out, along_out, n_out, a_sems, 1)()
    copies = []
    for d in y_order:
        copies.append(
            send(
                fo_all.at[gene],
                fo_all.at[gene],
                y_send.at[2, d - 1],
                y_recv.at[2, d - 1],
                along_y(d),
            )
        )
    settle(n_gene - 1)
    for copy in copies:
        copy.wait_recv()

    sizes = fo_all[n_gene - 1][:, chunk - 1 : chunk]
    portion = sizes / jnp.sum(sizes, axis=0, keepdims=True)

    def penalty_of(seen):
        ratio = (jnp.sum(seen, axis=0, keepdims=True) * portion + 1.0) / (seen + 1.0)
        return jnp.concatenate(split3(ratio * ratio), axis=0)

    for at in range(n_gene):
        pen3[:, at * chunk : (at + 1) * chunk] = penalty_of(fo_all[at])
    parts = dot(pen3[...], k_hi[...]) + dot(pen3[...], k_lo[...])
    parts = (parts[:B] + parts[B : 2 * B]) + parts[2 * B :]
    weighted = jnp.sum(parts * onehot, axis=0, keepdims=True)
    lane = lax.broadcasted_iota(jnp.int32, (1, wide), 1)
    weighted = jnp.where(lane < rows, weighted, 1.0)
    factor = dot_tn(penalty_of(fo_all[gene]), jnp.concatenate([hot, hot, hot], axis=0))
    kernel_own = kept_hi.astype(F32) + kept_lo.astype(F32)
    response = (kernel_own * factor * (1.0 / weighted)).astype(BF16)
    cs[...] = dot_nt(response, unit[...])
    fb_own[...] = dot_nt(hot, response)

    c_copies = []
    for d in in_order:
        to = lax.rem(inner + d, n_in)
        c_copies.append(
            send(
                cs.at[pl.ds(pl.multiple_of(to * piece, piece), piece)],
                cs_in.at[d - 1],
                c_send.at[0, d - 1],
                c_recv.at[0, d - 1],
                along_in(d),
            )
        )
    settle(n_in - 1)
    piece_sum = cs[pl.ds(pl.multiple_of(inner * piece, piece), piece), :]
    for d, copy in zip(in_order, c_copies):
        copy.wait_recv()
        piece_sum += cs_in[d - 1]
    cs_mid[...] = piece_sum
    cs_second = all_sum(cs_mid, cs_out, along_out, n_out, (c_send, c_recv), 1)
    fb_first = all_sum(fb_own, fb_in, along_in, n_in, a_sems, 2)
    fb_mid[...] = fb_first(n_in + n_out - 2)
    fb_second = all_sum(fb_mid, fb_out, along_out, n_out, a_sems, 3)
    piece_sum = cs_second(2 * (n_out - 1))
    length = jnp.sqrt(jnp.sum(piece_sum * piece_sum, axis=1, keepdims=True) + EPSILON)

    new_cent_ref[gene, inner] = piece_sum / length
    copies = []
    for d in y_order:
        copies.append(
            send(
                new_cent_ref.at[gene, inner],
                new_cent_ref.at[gene, inner],
                y_send.at[4, d - 1],
                y_recv.at[4, d - 1],
                along_y(d),
            )
        )

    def piece_to(d, e, target):
        rows_at = (lax.rem(gene + n_gene - d, n_gene), inner)
        return send(
            new_cent_ref.at[rows_at],
            new_cent_ref.at[rows_at],
            x_send.at[e, d],
            x_recv.at[e, d],
            target,
        )

    x_order = farthest_first(n_x)
    x_copies = [[piece_to(0, e, along_in(2 * e))] for e in x_order]
    obs_ref[gene] = fb_second(2 * n_gene + n_x)
    obs_copies = []
    for d in y_order:
        obs_copies.append(
            send(
                obs_ref.at[gene],
                obs_ref.at[gene],
                y_send.at[3, d - 1],
                y_recv.at[3, d - 1],
                along_y(d),
            )
        )
    for d, copy in reversed(list(zip(y_order, copies))):
        copy.wait_recv()
        for e, group in zip(x_order, x_copies):
            group.append(piece_to(d, e, along_in(2 * e)))

    def to_twin(number, at):
        column = new_cent_ref.at[:, number]
        return send(column, column, t_send.at[at], t_recv.at[at], twin)

    shared = [to_twin(inner, 0)]
    settle(n_gene * n_x)
    for e, group in zip(x_order, x_copies):
        for copy in group:
            copy.wait_recv()
        number = lax.rem(inner + n_in - 2 * e, n_in)
        shared.append(to_twin(number, e))
    for copy in obs_copies:
        copy.wait_recv()
    for at in range(n_gene):
        size = min(chunk, k_real - at * chunk)
        obs_out[:, at * chunk : at * chunk + size] = obs_ref[at][:, :size]
    settle(len(shared))
    for copy in shared:
        copy.wait_recv()
    settle(0)


def results_kernel(smooth_ref, cent_ref, obs_ref, smooth_out, cent_out, obs_out, sem):
    routes = (
        (cent_ref.at[pl.ds(0, cent_out.shape[0])], cent_out),
        (smooth_ref, smooth_out),
        (obs_ref, obs_out),
    )
    copies = [pltpu.make_async_copy(a, b, sem.at[at]) for at, (a, b) in enumerate(routes)]
    for copy in copies:
        copy.start()
    for copy in copies:
        copy.wait()


def shards(n_in, expression, gene_mean, loadings, nbr_index, nbr_count, nbr_weight, batch, centroids):
    rows = expression.shape[0]
    comps = loadings.shape[1]
    k_real = centroids.shape[0]
    n_gene = lax.axis_size("gene")
    n_out = lax.axis_size("cell") // n_in
    wide = padded(rows)
    k_wide = padded(k_real)
    share = comps // n_gene
    chunk = k_wide // n_gene
    piece = chunk // n_in
    vmem = pl.BlockSpec(memory_space=pltpu.VMEM)
    hbm = pl.BlockSpec(memory_space=pltpu.HBM)
    dims = (rows, k_real, n_gene, n_in, n_out)
    dma = pltpu.SemaphoreType.DMA
    smooth, new_cent, obs = pl.pallas_call(
        functools.partial(main_kernel, dims),
        out_shape=[
            pltpu.VMEM((share, rows), F32),
            pltpu.VMEM((n_gene, n_in, piece, comps), F32),
            pltpu.VMEM((B, k_real), F32),
        ],
        in_specs=[hbm, vmem, hbm, hbm, vmem, hbm, vmem, hbm],
        out_specs=[vmem] * 3,
        scratch_shapes=[
            pltpu.VMEM((n_gene, B, chunk), F32),
            pltpu.VMEM(expression.shape, BF16),
            pltpu.VMEM(loadings.shape, BF16),
            pltpu.VMEM((NBR, rows), jnp.int32),
            pltpu.VMEM((NBR, rows), F32),
            pltpu.VMEM(centroids.shape, F32),
            dma((5,)),
            pltpu.VMEM((comps, wide), F32),
            pltpu.VMEM((32, wide), jnp.int32),
            pltpu.VMEM((32, wide), F32),
            pltpu.VMEM((3 * wide, wide), BF16),
            pltpu.VMEM((3 * wide, wide), BF16),
            pltpu.VMEM((k_wide, comps), BF16),
            pltpu.VMEM((n_gene - 1, share, wide), F32),
            pltpu.VMEM((DIFF_STEPS, share, wide), F32),
            pltpu.VMEM((DIFF_STEPS, 2, share, wide), F32),
            pltpu.VMEM((comps, wide), F32),
            pltpu.VMEM((comps, wide), BF16),
            pltpu.VMEM((k_wide, wide), BF16),
            pltpu.VMEM((k_wide, wide), BF16),
            pltpu.VMEM((B, chunk), F32),
            pltpu.VMEM((max(n_in - 1, 1), B, chunk), F32),
            pltpu.VMEM((B, chunk), F32),
            pltpu.VMEM((max(n_out - 1, 1), B, chunk), F32),
            pltpu.VMEM((n_gene, B, chunk), F32),
            pltpu.VMEM((3 * B, k_wide), BF16),
            pltpu.VMEM((chunk, comps), F32),
            pltpu.VMEM((max(n_in - 1, 1), piece, comps), F32),
            pltpu.VMEM((piece, comps), F32),
            pltpu.VMEM((max(n_out - 1, 1), piece, comps), F32),
            pltpu.VMEM((B, chunk), F32),
            pltpu.VMEM((max(n_in - 1, 1), B, chunk), F32),
            pltpu.VMEM((B, chunk), F32),
            pltpu.VMEM((max(n_out - 1, 1), B, chunk), F32),
            dma((6, n_gene)),
            dma((6, n_gene)),
            dma((DIFF_STEPS, 2)),
            dma((DIFF_STEPS, 2)),
            dma((4, max(n_in, n_out) - 1)),
            dma((4, max(n_in, n_out) - 1)),
            dma((3, max(n_in, n_out) - 1)),
            dma((3, max(n_in, n_out) - 1)),
            dma((n_in // 2,)),
            dma((n_in // 2,)),
            dma((n_in // 2, n_gene)),
            dma((n_in // 2, n_gene)),
            pltpu.VMEM((2, share, wide), F32),
        ],
        compiler_params=pltpu.CompilerParams(
            collective_id=0, has_side_effects=True, vmem_limit_bytes=60 * 1024 * 1024
        ),
    )(
        expression,
        gene_mean,
        loadings,
        nbr_index.T,
        nbr_count,
        nbr_weight.T,
        batch,
        centroids,
    )

    smooth, new_cent, obs = pl.pallas_call(
        results_kernel,
        out_shape=[
            jax.ShapeDtypeStruct((share, rows), F32),
            jax.ShapeDtypeStruct((k_real, comps), F32),
            jax.ShapeDtypeStruct((B, k_real), F32),
        ],
        in_specs=[vmem] * 3,
        out_specs=[hbm] * 3,
        scratch_shapes=[dma((3,))],
        compiler_params=pltpu.CompilerParams(vmem_limit_bytes=32 * 1024 * 1024),
    )(smooth, new_cent.reshape(k_wide, comps), obs)
    return (smooth.T, new_cent, obs.T)


def solution(mesh):
    in_specs = (
        P("cell", "gene"),
        P("gene"),
        P("gene", None),
        P("cell", None),
        P("cell"),
        P("cell", None),
        P("cell"),
        P(),
    )
    out_specs = (P("cell", "gene"), P(), P())
    n_in = min(8, mesh.shape["cell"])
    body = functools.partial(shards, n_in)
    return jax.shard_map(body, mesh=mesh, in_specs=in_specs, out_specs=out_specs, check_vma=False)
```

```python
import functools

import jax
import jax.numpy as jnp
from jax import lax
from jax.experimental import pallas as pl
from jax.experimental.pallas import tpu as pltpu
from jax.sharding import PartitionSpec as P

B = 16
NBR = 30
DIFF_STEPS = 3
EPSILON = 1e-06
SIGMA_SCALE = 0.1
LANE = 128
MESH = pl.DeviceIdType.MESH
BF16 = jnp.bfloat16
F32 = jnp.float32


def padded(size, unit=LANE):
    return -(-size // unit) * unit


def split2(x):
    hi = x.astype(BF16)
    return hi, (x - hi.astype(F32)).astype(BF16)


def split3(x):
    hi = x.astype(BF16)
    rest = x - hi.astype(F32)
    mid = rest.astype(BF16)
    return hi, mid, (rest - mid.astype(F32)).astype(BF16)


def dot(a, b):
    return jnp.dot(a, b, preferred_element_type=F32)


def dot_nt(a, b):
    return lax.dot_general(a, b, (((1,), (1,)), ((), ())), preferred_element_type=F32)


def dot_tn(a, b):
    return lax.dot_general(a, b, (((0,), (0,)), ((), ())), preferred_element_type=F32)


def farthest_first(count):
    return sorted(range(1, count), key=lambda d: -min(d, count - d))


def build_weights(rows, block, index_ref, weight_ref, hi_ref, lo_ref, places=None):
    wide = hi_ref.shape[1]
    tile = LANE
    tiles = wide // tile
    base = block * wide
    for at in places or range(tiles):
        lanes = slice(at * tile, (at + 1) * tile)
        first, last = ((at, tiles), (0, tiles), (0, at + 1))[block]
        for low, high in ((0, first * tile), (min(last * tile, rows), wide)):
            if low < high:
                empty = jnp.zeros((high - low, tile), BF16)
                hi_ref[base + low : base + high, lanes] = empty
                lo_ref[base + low : base + high, lanes] = empty

        def rows_of(start, height, lanes=lanes):
            source = lax.broadcasted_iota(jnp.int32, (height, tile), 0) + (
                start + (block - 1) * rows
            )
            total = jnp.zeros((height, tile), F32)
            for slot in range(NBR):
                hit = index_ref[slot : slot + 1, lanes] == source
                total = jnp.where(hit, weight_ref[slot : slot + 1, lanes], total)
            hi, lo = split2(total)
            hi_ref[pl.ds(base + start, height), lanes] = hi
            lo_ref[pl.ds(base + start, height), lanes] = lo

        def fill(step, carry, rows_of=rows_of):
            rows_of(pl.multiple_of(step * tile, tile), tile)
            return carry

        lax.fori_loop(first, min(last, rows // tile), fill, 0)
        if last == tiles and rows % tile:
            rows_of(rows // tile * tile, rows % tile)


def main_kernel(
    dims,
    expr_hbm,
    mean_ref,
    load_hbm,
    index_hbm,
    count_ref,
    weight_hbm,
    batch_ref,
    centroid_hbm,
    smooth_ref,
    new_cent_ref,
    obs_out,
    obs_ref,
    expr_ref,
    load_ref,
    index_ref,
    weight_ref,
    centroid_ref,
    l_sem,
    part_ref,
    idx,
    wgt,
    w_hi,
    w_lo,
    cent_ref,
    rs_slots,
    state,
    halo,
    full,
    unit,
    k_hi,
    k_lo,
    fo_own,
    fo_in,
    fo_mid,
    fo_out,
    fo_all,
    pen3,
    cs,
    cs_in,
    cs_mid,
    cs_out,
    fb_own,
    fb_in,
    fb_mid,
    fb_out,
    y_send,
    y_recv,
    h_send,
    h_recv,
    a_send,
    a_recv,
    c_send,
    c_recv,
    t_send,
    t_recv,
    x_send,
    x_recv,
    turn,
):
    rows, k_real, n_gene, n_in, n_out = dims
    n_cell = n_in * n_out
    comps, wide = part_ref.shape
    y_order, in_order = farthest_first(n_gene), farthest_first(n_in)
    share = comps // n_gene
    chunk = cent_ref.shape[0] // n_gene
    piece = chunk // n_in
    n_x = n_in // 2
    cell = lax.axis_index("cell")
    gene = lax.axis_index("gene")
    inner = lax.rem(cell, n_in)
    outer = lax.div(cell, n_in)
    core = lax.rem(cell, 2)

    def along_y(d):
        return (cell, lax.rem(gene + d, n_gene))

    def along_in(d):
        return (outer * n_in + lax.rem(inner + d, n_in), gene)

    def along_out(d):
        return (lax.rem(outer + d, n_out) * n_in + inner, gene)

    after = (lax.rem(cell + 1, n_cell), gene)
    before = (lax.rem(cell + n_cell - 1, n_cell), gene)
    twin = (cell + 1 - 2 * core, gene)

    brought = [
        pltpu.make_async_copy(source, target, l_sem.at[at])
        for at, (source, target) in enumerate(
            (
                (load_hbm, load_ref),
                (expr_hbm, expr_ref),
                (index_hbm, index_ref),
                (weight_hbm, weight_ref),
                (centroid_hbm, centroid_ref),
            )
        )
    ]
    for copy in brought:
        copy.start()

    barrier = pltpu.get_barrier_semaphore()
    greeted = (
        [along_y(d) for d in range(1, n_gene)]
        + [along_in(d) for d in range(1, n_in)]
        + [along_out(d) for d in range(1, n_out)]
        + [after, before]
    )
    for target in greeted:
        pl.semaphore_signal(barrier, inc=1, device_id=target, device_id_type=MESH)

    mean = jnp.concatenate(
        [m.astype(F32) for m in split3(mean_ref[...][None, :])] + [jnp.zeros((5, mean_ref.shape[0]), F32)],
        axis=0,
    ).astype(BF16)
    brought[0].wait()
    turned = load_ref[...].T
    offset = jnp.sum(dot_nt(turned, mean), axis=1, keepdims=True)
    brought[1].wait()
    part_ref[:, rows:] = jnp.zeros((comps, wide - rows), F32)
    part_ref[:, :rows] = dot_nt(turned, expr_ref[...]) - offset
    pl.semaphore_wait(barrier, len(greeted))

    pending = []

    def send(src, dst, send_sem, recv_sem, target):
        copy = pltpu.make_async_remote_copy(
            src_ref=src,
            dst_ref=dst,
            send_sem=send_sem,
            recv_sem=recv_sem,
            device_id=target,
            device_id_type=MESH,
        )
        copy.start()
        pending.append(copy)
        return copy

    def settle(latest):
        while len(pending) > latest:
            pending.pop(0).wait_send()

    half = share // 2
    relay = n_gene == 8

    def share_of(d, start=0, size=share):
        at = lax.rem(gene + d, n_gene) * share + start
        return pl.ds(pl.multiple_of(at, half), size)

    own = share_of(0)
    routes = (
        (3, 0, half, 0, 1),
        (5, 0, half, 1, 7),
        (4, 0, half, 2, 2),
        (3, half, half, 0, 1),
        (5, half, half, 1, 7),
        (4, half, half, 2, 6),
        (1, 0, share, 3, 1),
        (7, 0, share, 4, 7),
    )
    if not relay:
        routes = tuple((d, 0, share, d - 1, d) for d in y_order)
    early = 6 if relay else len(routes)

    def send_route(at):
        d, start, size, slot, to = routes[at]
        return send(
            part_ref.at[share_of(d, start, size)],
            rs_slots.at[slot, pl.ds(start, size)],
            y_send.at[0, at],
            y_recv.at[0, at],
            along_y(to),
        )

    copies = [send_route(at) for at in range(early)]

    brought[2].wait()
    brought[3].wait()
    idx[...] = jnp.full(idx.shape, -(4 * rows), jnp.int32)
    idx[:NBR, :rows] = index_ref[...] - cell * rows
    live = lax.broadcasted_iota(jnp.int32, (NBR, rows), 0) < count_ref[...][None, :]
    kept = jnp.where(live, weight_ref[...], 0.0)
    wgt[...] = jnp.zeros_like(wgt)
    wgt[:NBR, :rows] = kept
    inverse = 1.0 / (1.0 + jnp.sum(wgt[...], axis=0, keepdims=True))
    merged = jnp.zeros(wgt.shape, F32)
    for slot in range(NBR):
        same = idx[...] == idx[slot : slot + 1, :]
        merged += jnp.where(same, wgt[slot : slot + 1, :], 0.0)
    wgt[...] = merged
    build_weights(rows, 1, idx, wgt, w_hi, w_lo, range(2))
    copies += [send_route(at) for at in range(early, len(routes))]

    def pass_on(part):
        for copy in copies[3 * part : 3 * part + 3]:
            copy.wait_recv()
        start = part * half
        place = slice(start, start + half)
        for at, d in enumerate((2, 6)):
            turn[at, place] = part_ref[share_of(d, start, half), :] + rs_slots[at, place]
        turn[part, place] += rs_slots[2, place]
        return [
            send(
                turn.at[at, pl.ds(start, half)],
                rs_slots.at[5 + at, pl.ds(start, half)],
                y_send.at[6, 2 * part + at],
                y_recv.at[6, 2 * part + at],
                along_y(d),
            )
            for at, d in enumerate((2, 6))
        ]

    passed = pass_on(0) if relay else []
    build_weights(rows, 1, idx, wgt, w_hi, w_lo, range(2, wide // LANE))
    if relay:
        passed += pass_on(1)
        copies = copies[6:] + passed
    build_weights(rows, 0, idx, wgt, w_hi, w_lo)
    brought[4].wait()
    cents = centroid_ref[...]
    cent_norm = jnp.sqrt(jnp.sum(cents * cents, axis=1, keepdims=True) + EPSILON)
    cent_ref[...] = jnp.concatenate(
        [cents / cent_norm, jnp.zeros((n_gene * chunk - k_real, comps), F32)], axis=0
    ).astype(BF16)
    onehot = jnp.concatenate(
        [
            (batch_ref[...][None, :] == lax.broadcasted_iota(jnp.int32, (B, rows), 0)).astype(F32),
            jnp.zeros((B, wide - rows), F32),
        ],
        axis=1,
    )
    counts = jnp.sum(onehot, axis=1, keepdims=True)
    hot = onehot.astype(BF16)

    value = part_ref[own, :]
    for copy in copies:
        copy.wait_recv()
    for slot in range(3 if relay else 0, n_gene - 1):
        value += rs_slots[slot]

    def spread(field, block):
        hi, lo = split2(field)
        pair = jnp.concatenate([hi, lo], axis=0)
        base = block * wide
        found = []
        for low in range(0, wide, 2 * LANE):
            high = min(low + 2 * LANE, wide)
            first, last = ((low, wide), (0, wide), (0, high))[block]
            span, lanes = slice(base + first, base + last), slice(low, high)
            both = dot(pair[:, first:last], w_hi[span, lanes])
            found.append(both[:share] + both[share:] + dot(hi[:, first:last], w_lo[span, lanes]))
        return jnp.concatenate(found, axis=1)

    for step in range(DIFF_STEPS):
        state[step] = value
        up = send(
            state.at[step], halo.at[step, 0], h_send.at[step, 0], h_recv.at[step, 0], after
        )
        down = send(
            state.at[step], halo.at[step, 1], h_send.at[step, 1], h_recv.at[step, 1], before
        )
        total = value + spread(value, 1)
        if step == 0:
            build_weights(rows, 2, idx, wgt, w_hi, w_lo)
        settle(2)
        up.wait_recv()
        total += spread(halo[step, 0], 0)
        down.wait_recv()
        total += spread(halo[step, 1], 2)
        value = total * inverse

    full[own, :] = value

    cut = padded(wide * 3 // 5)
    spans = ((0, cut), (cut, wide - cut))

    def share_to(target, at, rows_at, part):
        place = full.at[rows_at, pl.ds(*spans[part])]
        return send(place, place, y_send.at[1 + 4 * part, at], y_recv.at[1 + 4 * part, at], target)

    if relay:
        near = [
            [share_to(along_y(d), at, own, part) for at, d in enumerate((2, 6, 1, 7))]
            for part in range(2)
        ]
        arrivals = []
        for part in range(2):
            one, two = near[part][:2]
            one.wait_recv()
            far = [
                share_to(along_y(2), 4, share_of(6, half, half), part),
                share_to(along_y(1), 5, share_of(6), part),
            ]
            two.wait_recv()
            far.append(share_to(along_y(6), 6, share_of(2, 0, half), part))
            far.append(share_to(along_y(7), 7, share_of(2), part))
            arrivals.append(near[part][2:] + far)
    else:
        arrivals = [[share_to(along_y(d), d - 1, own, part) for d in y_order] for part in range(2)]

    smooth_ref[...] = value[:, :rows]

    settle(16 if relay else 2 * len(y_order))
    found = []
    for part in range(2):
        low, size = spans[part]
        lanes = slice(low, low + size)
        for copy in arrivals[part]:
            copy.wait_recv()
        whole = full[:, lanes]
        norm = jnp.sqrt(jnp.sum(whole * whole, axis=0, keepdims=True) + EPSILON)
        unit[:, lanes] = (whole * (1.0 / norm)).astype(BF16)

        def first(at, sums, lanes=lanes, size=size):
            start = pl.multiple_of(at * chunk, chunk)
            scores = dot(cent_ref[pl.ds(start, chunk), :], unit[:, lanes])
            number = lax.broadcasted_iota(jnp.int32, (chunk, size), 0) + start
            values = jnp.exp((scores - 1.0) * (2.0 / SIGMA_SCALE))
            values = jnp.where(number < k_real, values, 0.0)
            hi, lo = split2(values)
            k_hi[pl.ds(start, chunk), lanes] = hi
            k_lo[pl.ds(start, chunk), lanes] = lo
            return sums + jnp.sum(values, axis=0, keepdims=True)

        found.append(lax.fori_loop(0, n_gene, first, jnp.zeros((1, size), F32)))
    sums = jnp.concatenate(found, axis=1)
    mine = pl.multiple_of(gene * chunk, chunk)
    kept_hi, kept_lo = k_hi[pl.ds(mine, chunk), :], k_lo[pl.ds(mine, chunk), :]
    hi, lo = split2(onehot / sums)
    observed = dot_nt(hi, kept_hi) + dot_nt(lo, kept_hi) + dot_nt(hi, kept_lo)
    column = lax.broadcasted_iota(jnp.int32, (B, chunk), 1) + gene * chunk
    fo_own[...] = jnp.where(column == n_gene * chunk - 1, counts, observed)

    def all_sum(source, slots, target_of, count, sems, at):
        send_sem, recv_sem = sems
        copies = []
        for d in farthest_first(count):
            copies.append(
                send(
                    source,
                    slots.at[d - 1],
                    send_sem.at[at, d - 1],
                    recv_sem.at[at, d - 1],
                    target_of(d),
                )
            )

        def finish(latest=count - 1):
            settle(latest)
            total = source[...]
            for d, copy in zip(farthest_first(count), copies):
                copy.wait_recv()
                total += slots[d - 1]
            return total

        return finish

    a_sems = (a_send, a_recv)
    fo_mid[...] = all_sum(fo_own, fo_in, along_in, n_in, a_sems, 0)()
    fo_all[gene] = all_sum(fo_mid, fo_out, along_out, n_out, a_sems, 1)()
    copies = []
    for d in y_order:
        copies.append(
            send(
                fo_all.at[gene],
                fo_all.at[gene],
                y_send.at[2, d - 1],
                y_recv.at[2, d - 1],
                along_y(d),
            )
        )
    settle(n_gene - 1)
    for copy in copies:
        copy.wait_recv()

    sizes = fo_all[n_gene - 1][:, chunk - 1 : chunk]
    portion = sizes / jnp.sum(sizes, axis=0, keepdims=True)

    def penalty_of(seen):
        ratio = (jnp.sum(seen, axis=0, keepdims=True) * portion + 1.0) / (seen + 1.0)
        return jnp.concatenate(split3(ratio * ratio), axis=0)

    for at in range(n_gene):
        pen3[:, at * chunk : (at + 1) * chunk] = penalty_of(fo_all[at])
    parts = dot(pen3[...], k_hi[...]) + dot(pen3[...], k_lo[...])
    parts = (parts[:B] + parts[B : 2 * B]) + parts[2 * B :]
    weighted = jnp.sum(parts * onehot, axis=0, keepdims=True)
    lane = lax.broadcasted_iota(jnp.int32, (1, wide), 1)
    weighted = jnp.where(lane < rows, weighted, 1.0)
    factor = dot_tn(penalty_of(fo_all[gene]), jnp.concatenate([hot, hot, hot], axis=0))
    kernel_own = kept_hi.astype(F32) + kept_lo.astype(F32)
    response = (kernel_own * factor * (1.0 / weighted)).astype(BF16)
    cs[...] = dot_nt(response, unit[...])
    fb_own[...] = dot_nt(hot, response)

    c_copies = []
    for d in in_order:
        to = lax.rem(inner + d, n_in)
        c_copies.append(
            send(
                cs.at[pl.ds(pl.multiple_of(to * piece, piece), piece)],
                cs_in.at[d - 1],
                c_send.at[0, d - 1],
                c_recv.at[0, d - 1],
                along_in(d),
            )
        )
    settle(n_in - 1)
    piece_sum = cs[pl.ds(pl.multiple_of(inner * piece, piece), piece), :]
    for d, copy in zip(in_order, c_copies):
        copy.wait_recv()
        piece_sum += cs_in[d - 1]
    cs_mid[...] = piece_sum
    cs_second = all_sum(cs_mid, cs_out, along_out, n_out, (c_send, c_recv), 1)
    fb_first = all_sum(fb_own, fb_in, along_in, n_in, a_sems, 2)
    fb_mid[...] = fb_first(n_in + n_out - 2)
    fb_second = all_sum(fb_mid, fb_out, along_out, n_out, a_sems, 3)
    piece_sum = cs_second(2 * (n_out - 1))
    length = jnp.sqrt(jnp.sum(piece_sum * piece_sum, axis=1, keepdims=True) + EPSILON)

    new_cent_ref[gene, inner] = piece_sum / length
    copies = []
    for d in y_order:
        copies.append(
            send(
                new_cent_ref.at[gene, inner],
                new_cent_ref.at[gene, inner],
                y_send.at[4, d - 1],
                y_recv.at[4, d - 1],
                along_y(d),
            )
        )

    def piece_to(d, e, target):
        rows_at = (lax.rem(gene + n_gene - d, n_gene), inner)
        return send(
            new_cent_ref.at[rows_at],
            new_cent_ref.at[rows_at],
            x_send.at[e, d],
            x_recv.at[e, d],
            target,
        )

    x_order = farthest_first(n_x)
    x_copies = [[piece_to(0, e, along_in(2 * e))] for e in x_order]
    obs_ref[gene] = fb_second(2 * n_gene + n_x)
    obs_copies = []
    for d in y_order:
        obs_copies.append(
            send(
                obs_ref.at[gene],
                obs_ref.at[gene],
                y_send.at[3, d - 1],
                y_recv.at[3, d - 1],
                along_y(d),
            )
        )
    for d, copy in reversed(list(zip(y_order, copies))):
        copy.wait_recv()
        for e, group in zip(x_order, x_copies):
            group.append(piece_to(d, e, along_in(2 * e)))

    def to_twin(number, at):
        column = new_cent_ref.at[:, number]
        return send(column, column, t_send.at[at], t_recv.at[at], twin)

    shared = [to_twin(inner, 0)]
    settle(n_gene * n_x)
    for e, group in zip(x_order, x_copies):
        for copy in group:
            copy.wait_recv()
        number = lax.rem(inner + n_in - 2 * e, n_in)
        shared.append(to_twin(number, e))
    for copy in obs_copies:
        copy.wait_recv()
    for at in range(n_gene):
        size = min(chunk, k_real - at * chunk)
        obs_out[:, at * chunk : at * chunk + size] = obs_ref[at][:, :size]
    settle(len(shared))
    for copy in shared:
        copy.wait_recv()
    settle(0)


def results_kernel(smooth_ref, cent_ref, obs_ref, smooth_out, cent_out, obs_out, sem):
    routes = (
        (cent_ref.at[pl.ds(0, cent_out.shape[0])], cent_out),
        (smooth_ref, smooth_out),
        (obs_ref, obs_out),
    )
    copies = [pltpu.make_async_copy(a, b, sem.at[at]) for at, (a, b) in enumerate(routes)]
    for copy in copies:
        copy.start()
    for copy in copies:
        copy.wait()


def shards(n_in, expression, gene_mean, loadings, nbr_index, nbr_count, nbr_weight, batch, centroids):
    rows = expression.shape[0]
    comps = loadings.shape[1]
    k_real = centroids.shape[0]
    n_gene = lax.axis_size("gene")
    n_out = lax.axis_size("cell") // n_in
    wide = padded(rows)
    k_wide = padded(k_real)
    share = comps // n_gene
    chunk = k_wide // n_gene
    piece = chunk // n_in
    vmem = pl.BlockSpec(memory_space=pltpu.VMEM)
    hbm = pl.BlockSpec(memory_space=pltpu.HBM)
    dims = (rows, k_real, n_gene, n_in, n_out)
    dma = pltpu.SemaphoreType.DMA
    smooth, new_cent, obs = pl.pallas_call(
        functools.partial(main_kernel, dims),
        out_shape=[
            pltpu.VMEM((share, rows), F32),
            pltpu.VMEM((n_gene, n_in, piece, comps), F32),
            pltpu.VMEM((B, k_real), F32),
        ],
        in_specs=[hbm, vmem, hbm, hbm, vmem, hbm, vmem, hbm],
        out_specs=[vmem] * 3,
        scratch_shapes=[
            pltpu.VMEM((n_gene, B, chunk), F32),
            pltpu.VMEM(expression.shape, BF16),
            pltpu.VMEM(loadings.shape, BF16),
            pltpu.VMEM((NBR, rows), jnp.int32),
            pltpu.VMEM((NBR, rows), F32),
            pltpu.VMEM(centroids.shape, F32),
            dma((5,)),
            pltpu.VMEM((comps, wide), F32),
            pltpu.VMEM((32, wide), jnp.int32),
            pltpu.VMEM((32, wide), F32),
            pltpu.VMEM((3 * wide, wide), BF16),
            pltpu.VMEM((3 * wide, wide), BF16),
            pltpu.VMEM((k_wide, comps), BF16),
            pltpu.VMEM((n_gene - 1, share, wide), F32),
            pltpu.VMEM((DIFF_STEPS, share, wide), F32),
            pltpu.VMEM((DIFF_STEPS, 2, share, wide), F32),
            pltpu.VMEM((comps, wide), F32),
            pltpu.VMEM((comps, wide), BF16),
            pltpu.VMEM((k_wide, wide), BF16),
            pltpu.VMEM((k_wide, wide), BF16),
            pltpu.VMEM((B, chunk), F32),
            pltpu.VMEM((max(n_in - 1, 1), B, chunk), F32),
            pltpu.VMEM((B, chunk), F32),
            pltpu.VMEM((max(n_out - 1, 1), B, chunk), F32),
            pltpu.VMEM((n_gene, B, chunk), F32),
            pltpu.VMEM((3 * B, k_wide), BF16),
            pltpu.VMEM((chunk, comps), F32),
            pltpu.VMEM((max(n_in - 1, 1), piece, comps), F32),
            pltpu.VMEM((piece, comps), F32),
            pltpu.VMEM((max(n_out - 1, 1), piece, comps), F32),
            pltpu.VMEM((B, chunk), F32),
            pltpu.VMEM((max(n_in - 1, 1), B, chunk), F32),
            pltpu.VMEM((B, chunk), F32),
            pltpu.VMEM((max(n_out - 1, 1), B, chunk), F32),
            dma((7, n_gene)),
            dma((7, n_gene)),
            dma((DIFF_STEPS, 2)),
            dma((DIFF_STEPS, 2)),
            dma((4, max(n_in, n_out) - 1)),
            dma((4, max(n_in, n_out) - 1)),
            dma((3, max(n_in, n_out) - 1)),
            dma((3, max(n_in, n_out) - 1)),
            dma((n_in // 2,)),
            dma((n_in // 2,)),
            dma((n_in // 2, n_gene)),
            dma((n_in // 2, n_gene)),
            pltpu.VMEM((2, share, wide), F32),
        ],
        compiler_params=pltpu.CompilerParams(
            collective_id=0, has_side_effects=True, vmem_limit_bytes=60 * 1024 * 1024
        ),
    )(
        expression,
        gene_mean,
        loadings,
        nbr_index.T,
        nbr_count,
        nbr_weight.T,
        batch,
        centroids,
    )

    smooth, new_cent, obs = pl.pallas_call(
        results_kernel,
        out_shape=[
            jax.ShapeDtypeStruct((share, rows), F32),
            jax.ShapeDtypeStruct((k_real, comps), F32),
            jax.ShapeDtypeStruct((B, k_real), F32),
        ],
        in_specs=[vmem] * 3,
        out_specs=[hbm] * 3,
        scratch_shapes=[dma((3,))],
        compiler_params=pltpu.CompilerParams(vmem_limit_bytes=32 * 1024 * 1024),
    )(smooth, new_cent.reshape(k_wide, comps), obs)
    return (smooth.T, new_cent, obs.T)


def solution(mesh):
    in_specs = (
        P("cell", "gene"),
        P("gene"),
        P("gene", None),
        P("cell", None),
        P("cell"),
        P("cell", None),
        P("cell"),
        P(),
    )
    out_specs = (P("cell", "gene"), P(), P())
    n_in = min(8, mesh.shape["cell"])
    body = functools.partial(shards, n_in)
    return jax.shard_map(body, mesh=mesh, in_specs=in_specs, out_specs=out_specs, check_vma=False)
```
